512 devices in a mesh: group: 16 (over x_lo, y, core), dp: 32 (over z, x_hi).
Axes of the slice: x: 4 (x_hi: 2, x_lo: 2; x = x_hi * 2 + x_lo), y: 4, z: 16, core: 2. Of those that a mesh axis runs over, the one named last changes fastest.
Arguments:
- table: bfloat16 [262144, 1024], P(('group', 'dp')), may hold values from -6 to 6
- accum: float32 [262144], P(('group', 'dp')), may hold values from 0.05 to 5
- pair_block: int32 [262144], P(('group', 'dp')), may hold values from 0 to 2047, as said below
- pair_protein: int32 [262144], P(('group', 'dp')), may hold values from 0 to 2047, as said below
- pair_weight: bfloat16 [262144, 128], P(('group', 'dp')), may hold values from 0 to 1, as said below
- w_hidden: bfloat16 [1024, 1024], replicated, may hold values from -0.1875 to 0.1875
- hidden_cot: bfloat16 [2048, 1024], P(('group', 'dp')), may hold values from -6 to 6
Outputs:
- new_table: bfloat16 [262144, 1024], P(('group', 'dp'))
- new_accum: float32 [262144], P(('group', 'dp'))
The draws below stay inside these ranges and needn't reach their ends.
Inputs may be any that keep to these rules, and one draw needn't show every extreme that they name: `pair_block`: the owner of block b is device b // 4 along group+dp. Of one device's 512 pairs at most 2 name blocks of one owner; every device reaches 2 for some owner, and some owner receives 2 pairs from every device. `pair_protein`: A device's pairs name only that device's proteins (index // 4 is the device's index along group+dp), each of them at least once. `pair_weight`: Nonnegative; every pair has at least one positive weight.
All inputs are finite; a program needn't handle non-finite values.
Results may differ from the reference program's by a relative error of at most 0.001.
Values may be sent and summed in bfloat16 or wider, within the bound.
No kernel may reach another device: no remote copies, remote signals or barrier semaphores. Data moves between devices by JAX's collectives and lax.ppermute only.
A program may use at most 64 MiB of HBM per device.

```python
import math
import jax
import jax.numpy as jnp
from jax import lax

D = 1024
H = 1024
BLOCK = 128
BLK_DEV = 4
CAP = 2
P_DEV = 4
ROWS_DEV = 512
ROWS = 262144
PAIRS_DEV = 512
PAIRS = 262144
PROTEINS = 2048
N_GROUP = 16
N_DP = 32


def draw_pair_block(key, part):
    key = jax.random.fold_in(key, 11)
    count = N_GROUP * N_DP
    chosen = PAIRS_DEV // CAP
    key_hot, key_perm, key_local = jax.random.split(key, 3)
    hot_rank = jax.random.permutation(key_hot, count)
    hot_flag = (hot_rank < max(1, count // 16)).astype(jnp.int32)
    perms = jax.vmap(lambda k: jax.random.permutation(k, count))(jax.random.split(key_perm, count))
    scores = hot_flag[None, :] * count + perms.astype(jnp.int32)
    top_scores, owners = lax.top_k(scores, chosen)
    owners = jnp.repeat(owners.astype(jnp.int32), CAP, axis=1)
    local = jax.random.randint(key_local, (count, PAIRS_DEV), 0, BLK_DEV)
    return (owners * BLK_DEV + local).reshape(-1).astype(jnp.int32)


def draw_pair_protein(key, part):
    key = jax.random.fold_in(key, 12)
    count = N_GROUP * N_DP
    key_one, key_two = jax.random.split(key)
    first = jax.random.randint(key_one, (count, PAIRS_DEV), 0, P_DEV)
    second = jax.random.randint(key_two, (count, PAIRS_DEV), 0, P_DEV)
    local = jnp.minimum(first, second)
    local = local.at[:, :P_DEV].set(jnp.arange(P_DEV, dtype=jnp.int32)[None, :])
    offsets = jnp.arange(count, dtype=jnp.int32)[:, None] * P_DEV
    return (local + offsets).reshape(-1).astype(jnp.int32)


def draw_pair_weight(key, part):
    key = jax.random.fold_in(key, 13)
    key_keep, key_vals, key_first = jax.random.split(key, 3)
    sure_row = jax.random.randint(key_first, (PAIRS, 1), 0, BLOCK)
    columns = jnp.arange(BLOCK, dtype=jnp.int32)[None, :]
    keep = jax.random.bernoulli(key_keep, 0.02, (PAIRS, BLOCK)) | (columns == sure_row)
    values = jnp.exp(jax.random.uniform(key_vals, (PAIRS, BLOCK), jnp.float32, jnp.log(0.05), 0.0))
    return jnp.where(keep, values, 0.0).astype(jnp.float32).astype(jnp.bfloat16)


def level_of(rng, shape, pieces, low, largest):
    factor_of = 1.0
    for dim, shards_of in pieces:
        steps = jax.random.uniform(jax.random.fold_in(jax.random.fold_in(rng, 6), dim), (shards_of,), jnp.float32, low / len(pieces), largest / len(pieces))
        factor_of = factor_of * jnp.repeat(jnp.exp(steps), shape[dim] // shards_of).reshape((-1,) + (1,) * (len(shape) - 1 - dim))
    return factor_of


def noise(key, shape, scale, limit, shards=(), kind=jnp.bfloat16):
    level = level_of(key, shape, shards, -0.22, 0.18) if shards else 1.0
    result = jax.random.normal(key, shape, jnp.float32) * scale * level
    return jnp.minimum(jnp.maximum(result, -limit), limit).astype(kind)


def setup_inputs(seed: int = 0) -> dict:
    key_list = jax.random.split(jax.random.key(seed), 8)
    table = noise(key_list[0], (ROWS, D), 1.0, 6.0, ((0, 512),))
    accum = jnp.clip(jnp.exp(math.log(5.0) - 4.6051702 * jax.random.uniform(key_list[1], (ROWS,), jnp.float32) ** level_of(key_list[1], (ROWS,), ((0, 512),), -0.2, 0.2)), 0.05, 5.0)
    pair_block = draw_pair_block(jax.random.fold_in(key_list[7], 71), 0)
    pair_protein = draw_pair_protein(jax.random.fold_in(key_list[7], 71), 0)
    pair_weight = draw_pair_weight(jax.random.fold_in(key_list[7], 71), 0)
    w_hidden = noise(key_list[5], (D, H), D ** -0.5, 0.1875)
    hidden_cot = noise(key_list[6], (PROTEINS, H), 1.0, 6.0, ((0, 512),))
    return {"table": table, "accum": accum, "pair_block": pair_block, "pair_protein": pair_protein, "pair_weight": pair_weight, "w_hidden": w_hidden, "hidden_cot": hidden_cot}


def mlp_grad(bag, w_hidden, hidden_cot):
    inv = lax.rsqrt(lax.optimization_barrier(jnp.mean(bag * bag, axis=-1, keepdims=True)) + 1e-06)
    unit = bag * inv
    unit_b = unit.astype(jnp.bfloat16)
    pre = jnp.dot(unit_b, w_hidden, preferred_element_type=jnp.float32)
    sig = jax.nn.sigmoid(pre)
    dpre = (hidden_cot.astype(jnp.float32) * sig * (1.0 + pre * (1.0 - sig))).astype(jnp.bfloat16)
    dunit = lax.dot_general(dpre, w_hidden, (((1,), (1,)), ((), ())), preferred_element_type=jnp.float32)
    dbag = (dunit - unit * lax.optimization_barrier(jnp.mean(dunit * unit, axis=-1, keepdims=True))) * inv
    return dbag.astype(jnp.bfloat16)

def expand_dense(weights, blocks, count):
    hit = blocks[:, None, None] == jnp.arange(count, dtype=jnp.int32)[None, :, None]
    dense = jnp.where(hit, weights[:, None, :], jnp.zeros((), weights.dtype))
    return dense.reshape(weights.shape[0], count * weights.shape[1])

def reference(table, accum, pair_block, pair_protein, pair_weight, w_hidden, hidden_cot):
    devices = N_GROUP * N_DP
    slots = CAP * devices
    owner = (pair_block // BLK_DEV).astype(jnp.int32)
    order = jnp.argsort(owner, stable=True)
    s_owner = owner[order]
    s_blk = jnp.concatenate([(pair_block % BLK_DEV).astype(jnp.int32)[order], jnp.zeros((slots,), jnp.int32)])
    s_pid = jnp.concatenate([pair_protein.astype(jnp.int32)[order], jnp.zeros((slots,), jnp.int32)])
    s_w = jnp.concatenate([pair_weight[order], jnp.zeros((slots, BLOCK), pair_weight.dtype)])
    targets = jnp.arange(devices, dtype=jnp.int32)
    starts = jnp.searchsorted(s_owner, targets, side='left').astype(jnp.int32)
    ends = jnp.searchsorted(s_owner, targets, side='right').astype(jnp.int32)
    tables = table.reshape(devices, ROWS_DEV, D)
    accums = accum.reshape(devices, ROWS_DEV)

    def window(owner_id):
        begin = starts[owner_id]
        valid = begin + jnp.arange(slots, dtype=jnp.int32) < ends[owner_id]
        weights = lax.dynamic_slice(s_w, (begin, jnp.int32(0)), (slots, BLOCK))
        weights = jnp.where(valid[:, None], weights, jnp.zeros((), weights.dtype))
        blocks = lax.dynamic_slice(s_blk, (begin,), (slots,))
        pids = lax.dynamic_slice(s_pid, (begin,), (slots,))
        return (expand_dense(weights, blocks, BLK_DEV), pids, valid)

    def forward(bag, inputs):
        owner_id, rows = inputs
        dense, pids, valid = window(owner_id)
        partial_value = jnp.dot(dense, rows, preferred_element_type=jnp.float32).astype(jnp.bfloat16).astype(jnp.float32)
        partial_value = jnp.where(valid[:, None], partial_value, jnp.zeros((), jnp.float32))
        return (bag.at[pids].add(partial_value), None)
    bag, _ = lax.scan(forward, jnp.zeros((PROTEINS, D), jnp.float32), (targets, tables))
    dbag = mlp_grad(bag, w_hidden, hidden_cot)

    def backward(inputs):
        owner_id, rows, acc = inputs
        dense, pids, valid = window(owner_id)
        grads = dbag[pids]
        grad = lax.dot_general(dense, grads, (((0,), (0,)), ((), ())), preferred_element_type=jnp.float32)
        acc_new = acc + lax.optimization_barrier(jnp.mean(grad * grad, axis=-1))
        rows_new = rows.astype(jnp.float32) - 0.3 * grad / (jnp.sqrt(acc_new)[:, None] + 1e-08)
        return (rows_new.astype(jnp.bfloat16), acc_new)
    new_rows, new_acc = lax.map(backward, (targets, tables, accums))
    return (new_rows.reshape(ROWS, D), new_acc.reshape(ROWS))
```

```python
import jax
import jax.numpy as jnp
from jax import lax
from jax.sharding import Mesh
from jax.sharding import PartitionSpec as P

CAP = 2
AXES = ("xl", "y", "c", "z", "xh")
SIZES = (2, 4, 2, 16, 2)
PLANE = ("xl", "y", "c", "xh")


def mlp_grad(bag, w_hidden, hidden_cot):
    inv = lax.rsqrt(jnp.mean(bag * bag, axis=-1, keepdims=True) + 1e-06)
    unit = bag * inv
    unit_b = unit.astype(jnp.bfloat16)
    pre = jnp.dot(unit_b, w_hidden, preferred_element_type=jnp.float32)
    sig = jax.nn.sigmoid(pre)
    dpre = (hidden_cot.astype(jnp.float32) * sig * (1.0 + pre * (1.0 - sig))).astype(jnp.bfloat16)
    dunit = lax.dot_general(
        dpre, w_hidden, (((1,), (1,)), ((), ())), preferred_element_type=jnp.float32
    )
    dbag = (dunit - unit * jnp.mean(dunit * unit, axis=-1, keepdims=True)) * inv
    return dbag.astype(jnp.bfloat16)


def exchange(x, axes):
    return lax.all_to_all(x, axes, split_axis=0, concat_axis=0, tiled=True)


def per_device(table, accum, pair_block, pair_protein, pair_weight, w_hidden, hidden_cot):
    nz = lax.axis_size("z")
    nh = lax.axis_size("xh")
    devices = lax.axis_size(AXES)
    npl = devices // nz
    n_dp = nz * nh
    rows_dev, width = table.shape
    block_rows = pair_weight.shape[1]
    blocks_dev = rows_dev // block_rows
    pairs = pair_block.shape[0]
    proteins = hidden_cot.shape[0]
    slots = CAP * devices
    device_id = lax.axis_index(AXES)

    owner = pair_block // blocks_dev
    local_block = pair_block % blocks_dev
    local_prot = pair_protein - device_id * proteins
    positions = jnp.arange(pairs, dtype=jnp.int32)
    earlier = (owner[:, None] == owner[None, :]) & (positions[None, :] < positions[:, None])
    rank = jnp.sum(earlier.astype(jnp.int32), axis=1)
    oz = (owner % n_dp) // nh
    opl = (owner // n_dp) * nh + owner % nh
    slot = (oz * npl + opl) * CAP + rank
    code = local_prot * blocks_dev + local_block + 1
    place = slot[None, :] == jnp.arange(slots, dtype=jnp.int32)[:, None]
    send_w = jnp.dot(
        place.astype(jnp.bfloat16), pair_weight, preferred_element_type=jnp.float32
    ).astype(jnp.bfloat16)
    send_code = jnp.max(jnp.where(place, code[None, :], 0), axis=1)

    per_z = npl * CAP
    code_rows = jnp.pad(
        send_code.reshape(nz, 1, per_z).astype(jnp.bfloat16),
        ((0, 0), (0, 7), (0, block_rows - per_z)),
    )
    got1 = exchange(
        jnp.concatenate([send_w.reshape(nz, per_z, block_rows), code_rows], axis=1), "z"
    )
    w1 = got1[:, :per_z].reshape(nz, npl, CAP, block_rows)
    code1 = got1[:, per_z, :per_z].astype(jnp.int32).reshape(nz, npl, CAP)
    code1 = code1.transpose(1, 0, 2) - 1
    w1 = w1.transpose(1, 0, 2, 3)

    per_p = nz * CAP
    blk1 = (code1 & (blocks_dev - 1)).astype(jnp.bfloat16)
    blk_rows = jnp.pad(
        blk1.reshape(npl, 1, per_p), ((0, 0), (0, 7), (0, block_rows - per_p))
    )
    got2 = exchange(
        jnp.concatenate([w1.reshape(npl, per_p, block_rows), blk_rows], axis=1), PLANE
    )
    w2 = got2[:, :per_p].reshape(slots, block_rows)
    blk2 = got2[:, per_p, :per_p].astype(jnp.int32).reshape(slots)
    hit = blk2[:, None, None] == jnp.arange(blocks_dev, dtype=jnp.int32)[None, :, None]
    dense = jnp.where(hit, w2[:, None, :], jnp.zeros((), jnp.bfloat16)).reshape(slots, rows_dev)
    partial_value = jnp.dot(dense, table, preferred_element_type=jnp.float32).astype(jnp.bfloat16)

    got3 = exchange(partial_value.reshape(npl, per_p, width), PLANE).reshape(slots, width)
    prot1 = lax.shift_right_arithmetic(code1, blocks_dev.bit_length() - 1)
    zs = jnp.arange(nz, dtype=jnp.int32)
    target = prot1 + jnp.where(prot1 >= 0, zs[None, :, None] * proteins, 0)
    member = (
        target.reshape(1, slots) == jnp.arange(nz * proteins, dtype=jnp.int32)[:, None]
    ).astype(jnp.bfloat16)
    bag_part = jnp.dot(member, got3, preferred_element_type=jnp.float32)
    bag = jnp.sum(exchange(bag_part.reshape(nz, proteins, width), "z"), axis=0)

    dbag = mlp_grad(bag, w_hidden, hidden_cot)

    every = exchange(jnp.broadcast_to(dbag[None], (nz, proteins, width)), "z")
    every = every.reshape(nz * proteins, width)
    send_g = lax.dot_general(
        member, every, (((0,), (0,)), ((), ())), preferred_element_type=jnp.float32
    ).astype(jnp.bfloat16)
    got_grad = exchange(send_g.reshape(npl, per_p, width), PLANE).reshape(slots, width)
    grad = lax.dot_general(
        dense, got_grad, (((0,), (0,)), ((), ())), preferred_element_type=jnp.float32
    )
    acc_new = accum + jnp.mean(grad * grad, axis=-1)
    rows_new = table.astype(jnp.float32) - 0.3 * grad / (jnp.sqrt(acc_new)[:, None] + 1e-08)
    return (rows_new.astype(jnp.bfloat16), acc_new)


def solution(mesh):
    split = Mesh(mesh.devices.reshape(SIZES), AXES)
    in_specs = (
        P(AXES, None),
        P(AXES),
        P(AXES),
        P(AXES),
        P(AXES, None),
        P(),
        P(AXES, None),
    )
    out_specs = (P(AXES, None), P(AXES))
    return jax.shard_map(
        per_device, mesh=split, in_specs=in_specs, out_specs=out_specs, check_vma=False
    )
```

```python
import jax
import jax.numpy as jnp
from jax import lax
from jax.experimental import pallas as pl
from jax.experimental.pallas import tpu as pltpu
from jax.sharding import Mesh
from jax.sharding import PartitionSpec as P

CAP = 2
AXES = ("xl", "y", "c", "z", "xh")
SIZES = (2, 4, 2, 16, 2)
PLANE = ("xl", "y", "c", "xh")


def mlp_grad(bag, w_hidden, hidden_cot):
    inv = lax.rsqrt(jnp.mean(bag * bag, axis=-1, keepdims=True) + 1e-06)
    unit = bag * inv
    unit_b = unit.astype(jnp.bfloat16)
    pre = jnp.dot(unit_b, w_hidden, preferred_element_type=jnp.float32)
    sig = jax.nn.sigmoid(pre)
    dpre = (hidden_cot.astype(jnp.float32) * sig * (1.0 + pre * (1.0 - sig))).astype(jnp.bfloat16)
    dunit = lax.dot_general(
        dpre, w_hidden, (((1,), (1,)), ((), ())), preferred_element_type=jnp.float32
    )
    dbag = (dunit - unit * jnp.mean(dunit * unit, axis=-1, keepdims=True)) * inv
    return dbag.astype(jnp.bfloat16)


def owner_kernel(got_ref, table_ref, partial_ref, dense_ref):
    groups, _, block_rows = got_ref.shape
    per_p = partial_ref.shape[1]
    blocks_dev = table_ref.shape[0] // block_rows
    width = table_ref.shape[1]
    got = got_ref[...].astype(jnp.float32)
    row = got[:, per_p : per_p + 1, :]
    shape = (groups, per_p, block_rows)
    diagonal = lax.broadcasted_iota(jnp.int32, shape, 1) == lax.broadcasted_iota(
        jnp.int32, shape, 2
    )
    block = jnp.sum(jnp.where(diagonal, row, 0.0), axis=2, keepdims=True)
    weights = got[:, :per_p, :]
    for b in range(blocks_dev):
        mine = jnp.where(block == b, weights, 0.0).astype(jnp.bfloat16)
        dense_ref[:, b * block_rows : (b + 1) * block_rows] = mine.reshape(
            groups * per_p, block_rows
        )
    partial_ref[...] = (
        jnp.dot(dense_ref[...], table_ref[...], preferred_element_type=jnp.float32)
        .astype(jnp.bfloat16)
        .reshape(groups, per_p, width)
    )


def owner_partials(got, table, per_p):
    npl, rows, block_rows = got.shape
    rows_dev, width = table.shape
    step = 8
    return pl.pallas_call(
        owner_kernel,
        grid=(npl // step,),
        in_specs=[
            pl.BlockSpec((step, rows, block_rows), lambda i: (i, 0, 0)),
            pl.BlockSpec((rows_dev, width), lambda i: (0, 0)),
        ],
        out_specs=[
            pl.BlockSpec((step, per_p, width), lambda i: (i, 0, 0)),
            pl.BlockSpec((step * per_p, rows_dev), lambda i: (i, 0)),
        ],
        out_shape=[
            jax.ShapeDtypeStruct((npl, per_p, width), jnp.bfloat16),
            jax.ShapeDtypeStruct((npl * per_p, rows_dev), jnp.bfloat16),
        ],
        compiler_params=pltpu.CompilerParams(vmem_limit_bytes=24 * 2**20),
        name="owner_partials",
    )(got, table)


def exchange(x, axes):
    return lax.all_to_all(x, axes, split_axis=0, concat_axis=0, tiled=True)


def per_device(table, accum, pair_block, pair_protein, pair_weight, w_hidden, hidden_cot):
    nz = lax.axis_size("z")
    nh = lax.axis_size("xh")
    devices = lax.axis_size(AXES)
    npl = devices // nz
    n_dp = nz * nh
    rows_dev, width = table.shape
    block_rows = pair_weight.shape[1]
    blocks_dev = rows_dev // block_rows
    pairs = pair_block.shape[0]
    proteins = hidden_cot.shape[0]
    slots = CAP * devices
    device_id = lax.axis_index(AXES)

    owner = pair_block // blocks_dev
    local_block = pair_block % blocks_dev
    local_prot = pair_protein - device_id * proteins
    positions = jnp.arange(pairs, dtype=jnp.int32)
    earlier = (owner[:, None] == owner[None, :]) & (positions[None, :] < positions[:, None])
    rank = jnp.sum(earlier.astype(jnp.int32), axis=1)
    oz = (owner % n_dp) // nh
    opl = (owner // n_dp) * nh + owner % nh
    slot = (oz * npl + opl) * CAP + rank
    code = local_prot * blocks_dev + local_block + 1
    place = slot[None, :] == jnp.arange(slots, dtype=jnp.int32)[:, None]
    send_w = jnp.dot(
        place.astype(jnp.bfloat16), pair_weight, preferred_element_type=jnp.float32
    ).astype(jnp.bfloat16)
    send_code = jnp.max(jnp.where(place, code[None, :], 0), axis=1)

    per_z = npl * CAP
    code_rows = jnp.pad(
        send_code.reshape(nz, 1, per_z).astype(jnp.bfloat16),
        ((0, 0), (0, 7), (0, block_rows - per_z)),
    )
    got1 = exchange(
        jnp.concatenate([send_w.reshape(nz, per_z, block_rows), code_rows], axis=1), "z"
    )
    w1 = got1[:, :per_z].reshape(nz, npl, CAP, block_rows)
    code1 = got1[:, per_z, :per_z].astype(jnp.int32).reshape(nz, npl, CAP)
    code1 = code1.transpose(1, 0, 2) - 1
    w1 = w1.transpose(1, 0, 2, 3)

    per_p = nz * CAP
    blk1 = (code1 & (blocks_dev - 1)).astype(jnp.bfloat16)
    blk_rows = jnp.pad(
        blk1.reshape(npl, 1, per_p), ((0, 0), (0, 7), (0, block_rows - per_p))
    )
    got2 = exchange(
        jnp.concatenate([w1.reshape(npl, per_p, block_rows), blk_rows], axis=1), PLANE
    )
    partial_value, dense = owner_partials(got2, table, per_p)

    got3 = exchange(partial_value, PLANE).reshape(slots, width)
    prot1 = lax.shift_right_arithmetic(code1, blocks_dev.bit_length() - 1)
    zs = jnp.arange(nz, dtype=jnp.int32)
    target = prot1 + jnp.where(prot1 >= 0, zs[None, :, None] * proteins, 0)
    member = (
        target.reshape(1, slots) == jnp.arange(nz * proteins, dtype=jnp.int32)[:, None]
    ).astype(jnp.bfloat16)
    bag_part = jnp.dot(member, got3, preferred_element_type=jnp.float32)
    bag = jnp.sum(exchange(bag_part.reshape(nz, proteins, width), "z"), axis=0)

    dbag = mlp_grad(bag, w_hidden, hidden_cot)

    every = exchange(jnp.broadcast_to(dbag[None], (nz, proteins, width)), "z")
    every = every.reshape(nz * proteins, width)
    send_g = lax.dot_general(
        member, every, (((0,), (0,)), ((), ())), preferred_element_type=jnp.float32
    ).astype(jnp.bfloat16)
    got_grad = exchange(send_g.reshape(npl, per_p, width), PLANE).reshape(slots, width)
    grad = lax.dot_general(
        dense, got_grad, (((0,), (0,)), ((), ())), preferred_element_type=jnp.float32
    )
    acc_new = accum + jnp.mean(grad * grad, axis=-1)
    rows_new = table.astype(jnp.float32) - 0.3 * grad / (jnp.sqrt(acc_new)[:, None] + 1e-08)
    return (rows_new.astype(jnp.bfloat16), acc_new)


def solution(mesh):
    split = Mesh(mesh.devices.reshape(SIZES), AXES)
    in_specs = (
        P(AXES, None),
        P(AXES),
        P(AXES),
        P(AXES),
        P(AXES, None),
        P(),
        P(AXES, None),
    )
    out_specs = (P(AXES, None), P(AXES))
    return jax.shard_map(
        per_device, mesh=split, in_specs=in_specs, out_specs=out_specs, check_vma=False
    )
```

```python
import jax
import jax.numpy as jnp
from jax import lax
from jax.experimental import pallas as pl
from jax.experimental.pallas import tpu as pltpu
from jax.sharding import Mesh
from jax.sharding import PartitionSpec as P

CAP = 2
AXES = ("xl", "y", "c", "z", "xh")
SIZES = (2, 4, 2, 16, 2)
PLANE = ("xl", "y", "c", "xh")


def mlp_grad(bag, w_hidden, hidden_cot):
    inv = lax.rsqrt(jnp.mean(bag * bag, axis=-1, keepdims=True) + 1e-06)
    unit = bag * inv
    unit_b = unit.astype(jnp.bfloat16)
    pre = jnp.dot(unit_b, w_hidden, preferred_element_type=jnp.float32)
    sig = jax.nn.sigmoid(pre)
    dpre = (hidden_cot.astype(jnp.float32) * sig * (1.0 + pre * (1.0 - sig))).astype(jnp.bfloat16)
    dunit = lax.dot_general(
        dpre, w_hidden, (((1,), (1,)), ((), ())), preferred_element_type=jnp.float32
    )
    dbag = (dunit - unit * jnp.mean(dunit * unit, axis=-1, keepdims=True)) * inv
    return dbag.astype(jnp.bfloat16)


def slot_blocks(got, per_p):
    shape = (got.shape[0], per_p, got.shape[2])
    diagonal = lax.broadcasted_iota(jnp.int32, shape, 1) == lax.broadcasted_iota(
        jnp.int32, shape, 2
    )
    row = got[:, per_p : per_p + 1, :]
    return jnp.sum(jnp.where(diagonal, row, 0.0), axis=2, keepdims=True)


def owner_kernel(got_ref, target_ref, table_ref, partial_ref, member_ref, dense_ref):
    protein = lax.broadcasted_iota(jnp.int32, member_ref.shape, 0)
    member_ref[...] = jnp.where(target_ref[...] == protein, 1.0, 0.0).astype(jnp.bfloat16)
    groups, per_p, width = partial_ref.shape
    block_rows = got_ref.shape[2]
    got = got_ref[...].astype(jnp.float32)
    block = slot_blocks(got, per_p)
    weights = got[:, :per_p, :]
    for b in range(table_ref.shape[0] // block_rows):
        mine = jnp.where(block == b, weights, 0.0).astype(jnp.bfloat16)
        dense_ref[:, b * block_rows : (b + 1) * block_rows] = mine.reshape(
            groups * per_p, block_rows
        )
    partial_ref[...] = (
        jnp.dot(dense_ref[...], table_ref[...], preferred_element_type=jnp.float32)
        .astype(jnp.bfloat16)
        .reshape(groups, per_p, width)
    )


def update_kernel(got_ref, grad_ref, table_ref, accum_ref, table_out, accum_out):
    groups, per_p, width = grad_ref.shape
    block_rows = got_ref.shape[2]
    got = got_ref[...].astype(jnp.float32)
    mine = jnp.where(slot_blocks(got, per_p) == pl.program_id(0), got[:, :per_p, :], 0.0)
    grad = lax.dot_general(
        mine.astype(jnp.bfloat16).reshape(groups * per_p, block_rows),
        grad_ref[...].reshape(groups * per_p, width),
        (((0,), (0,)), ((), ())),
        preferred_element_type=jnp.float32,
    )
    square = (block_rows, block_rows)
    diagonal = lax.broadcasted_iota(jnp.int32, square, 0) == lax.broadcasted_iota(
        jnp.int32, square, 1
    )
    accum = jnp.sum(jnp.where(diagonal, accum_ref[0], 0.0), axis=1, keepdims=True)
    accum = accum + jnp.mean(grad * grad, axis=1, keepdims=True)
    rate = 0.3 / (jnp.sqrt(accum) + 1e-08)
    table_out[...] = (table_ref[...].astype(jnp.float32) - grad * rate).astype(jnp.bfloat16)
    accum_out[0] = jnp.sum(jnp.where(diagonal, accum, 0.0), axis=0, keepdims=True)


def update_rows(got, grad, table, accum):
    npl, rows, block_rows = got.shape
    _, per_p, width = grad.shape
    blocks = table.shape[0] // block_rows
    whole = lambda i: (0, 0, 0)
    table_spec = pl.BlockSpec((block_rows, width), lambda i: (i, 0))
    accum_spec = pl.BlockSpec((1, 1, block_rows), lambda i: (i, 0, 0))
    new_table, new_accum = pl.pallas_call(
        update_kernel,
        grid=(blocks,),
        in_specs=[
            pl.BlockSpec(got.shape, whole),
            pl.BlockSpec(grad.shape, whole),
            table_spec,
            accum_spec,
        ],
        out_specs=[table_spec, accum_spec],
        out_shape=[
            jax.ShapeDtypeStruct(table.shape, table.dtype),
            jax.ShapeDtypeStruct((blocks, 1, block_rows), jnp.float32),
        ],
        compiler_params=pltpu.CompilerParams(vmem_limit_bytes=24 * 2**20),
        name="update_rows",
    )(got, grad, table, accum.reshape(blocks, 1, block_rows))
    return new_table, new_accum.reshape(accum.shape)


def owner_partials(got, target, table, per_p, sums):
    npl, rows, block_rows = got.shape
    rows_dev, width = table.shape
    step = 8
    return pl.pallas_call(
        owner_kernel,
        grid=(npl // step,),
        in_specs=[
            pl.BlockSpec((step, rows, block_rows), lambda i: (i, 0, 0)),
            pl.BlockSpec((1, step * per_p), lambda i: (0, i)),
            pl.BlockSpec((rows_dev, width), lambda i: (0, 0)),
        ],
        out_specs=[
            pl.BlockSpec((step, per_p, width), lambda i: (i, 0, 0)),
            pl.BlockSpec((sums, step * per_p), lambda i: (0, i)),
        ],
        out_shape=[
            jax.ShapeDtypeStruct((npl, per_p, width), jnp.bfloat16),
            jax.ShapeDtypeStruct((sums, npl * per_p), jnp.bfloat16),
        ],
        scratch_shapes=[pltpu.VMEM((step * per_p, rows_dev), jnp.bfloat16)],
        compiler_params=pltpu.CompilerParams(vmem_limit_bytes=24 * 2**20),
        name="owner_partials",
    )(got, target, table)


def sum_kernel(member_ref, got_ref, out_ref):
    slots = got_ref.shape[0] * got_ref.shape[1]
    total = jnp.dot(
        member_ref[...],
        got_ref[...].reshape(slots, got_ref.shape[2]),
        preferred_element_type=jnp.float32,
    )
    out_ref[...] = total.reshape(out_ref.shape)


def protein_sums(member, got, nz):
    sums, slots = member.shape
    npl, per_p, width = got.shape
    step = 256
    return pl.pallas_call(
        sum_kernel,
        grid=(width // step,),
        in_specs=[
            pl.BlockSpec((sums, slots), lambda i: (0, 0)),
            pl.BlockSpec((npl, per_p, step), lambda i: (0, 0, i)),
        ],
        out_specs=pl.BlockSpec((nz, sums // nz, step), lambda i: (0, 0, i)),
        out_shape=jax.ShapeDtypeStruct((nz, sums // nz, width), jnp.float32),
        compiler_params=pltpu.CompilerParams(vmem_limit_bytes=16 * 2**20),
        name="protein_sums",
    )(member, got)


def exchange(x, axes):
    return lax.all_to_all(x, axes, split_axis=0, concat_axis=0, tiled=True)


def per_device(table, accum, pair_block, pair_protein, pair_weight, w_hidden, hidden_cot):
    nz = lax.axis_size("z")
    nh = lax.axis_size("xh")
    devices = lax.axis_size(AXES)
    npl = devices // nz
    n_dp = nz * nh
    rows_dev, width = table.shape
    block_rows = pair_weight.shape[1]
    blocks_dev = rows_dev // block_rows
    pairs = pair_block.shape[0]
    proteins = hidden_cot.shape[0]
    slots = CAP * devices
    device_id = lax.axis_index(AXES)

    owner = pair_block // blocks_dev
    local_block = pair_block % blocks_dev
    local_prot = pair_protein - device_id * proteins
    positions = jnp.arange(pairs, dtype=jnp.int32)
    earlier = (owner[:, None] == owner[None, :]) & (positions[None, :] < positions[:, None])
    rank = jnp.sum(earlier.astype(jnp.int32), axis=1)
    oz = (owner % n_dp) // nh
    opl = (owner // n_dp) * nh + owner % nh
    slot = (oz * npl + opl) * CAP + rank
    code = local_prot * blocks_dev + local_block + 1
    place = slot[None, :] == jnp.arange(slots, dtype=jnp.int32)[:, None]
    send_w = jnp.dot(
        place.astype(jnp.bfloat16), pair_weight, preferred_element_type=jnp.float32
    ).astype(jnp.bfloat16)
    send_code = jnp.max(jnp.where(place, code[None, :], 0), axis=1)

    per_z = npl * CAP
    code_rows = jnp.pad(
        send_code.reshape(nz, 1, per_z).astype(jnp.bfloat16),
        ((0, 0), (0, 7), (0, block_rows - per_z)),
    )
    got1 = exchange(
        jnp.concatenate([send_w.reshape(nz, per_z, block_rows), code_rows], axis=1), "z"
    )
    w1 = got1[:, :per_z].reshape(nz, npl, CAP, block_rows)
    code1 = got1[:, per_z, :per_z].astype(jnp.int32).reshape(nz, npl, CAP)
    code1 = code1.transpose(1, 0, 2) - 1
    w1 = w1.transpose(1, 0, 2, 3)

    per_p = nz * CAP
    blk1 = (code1 & (blocks_dev - 1)).astype(jnp.bfloat16)
    blk_rows = jnp.pad(
        blk1.reshape(npl, 1, per_p), ((0, 0), (0, 7), (0, block_rows - per_p))
    )
    got2 = exchange(
        jnp.concatenate([w1.reshape(npl, per_p, block_rows), blk_rows], axis=1), PLANE
    )
    prot1 = lax.shift_right_arithmetic(code1, blocks_dev.bit_length() - 1)
    zs = jnp.arange(nz, dtype=jnp.int32)
    target = prot1 + jnp.where(prot1 >= 0, zs[None, :, None] * proteins, 0)
    partial_value, member = owner_partials(
        got2, target.reshape(1, slots), table, per_p, nz * proteins
    )

    bag_part = protein_sums(member, exchange(partial_value, PLANE), nz)
    bag = jnp.sum(exchange(bag_part, "z"), axis=0)

    dbag = mlp_grad(bag, w_hidden, hidden_cot)

    every = exchange(jnp.broadcast_to(dbag[None], (nz, proteins, width)), "z")
    every = every.reshape(nz * proteins, width)
    send_g = lax.dot_general(
        member, every, (((0,), (0,)), ((), ())), preferred_element_type=jnp.float32
    ).astype(jnp.bfloat16)
    got_grad = exchange(send_g.reshape(npl, per_p, width), PLANE)
    return update_rows(got2, got_grad, table, accum)


def solution(mesh):
    split = Mesh(mesh.devices.reshape(SIZES), AXES)
    in_specs = (
        P(AXES, None),
        P(AXES),
        P(AXES),
        P(AXES),
        P(AXES, None),
        P(),
        P(AXES, None),
    )
    out_specs = (P(AXES, None), P(AXES))
    return jax.shard_map(
        per_device, mesh=split, in_specs=in_specs, out_specs=out_specs, check_vma=False
    )
```

```python
import functools

import jax
import jax.numpy as jnp
from jax import lax
from jax.experimental import pallas as pl
from jax.experimental.pallas import tpu as pltpu
from jax.sharding import Mesh
from jax.sharding import PartitionSpec as P

CAP = 2
BLK_DEV = 4
AXES = ("xl", "y", "c", "z", "xh")
SIZES = (2, 4, 2, 16, 2)
PLANE = ("xl", "y", "c", "xh")


def dense_layer_kernel(sums_ref, w_ref, cot_ref, out_ref):
    nz = sums_ref.shape[0]
    bag = sums_ref[0]
    for z in range(1, nz):
        bag = bag + sums_ref[z]
    inv = lax.rsqrt(jnp.mean(bag * bag, axis=-1, keepdims=True) + 1e-06)
    unit = bag * inv
    pre = jnp.dot(unit.astype(jnp.bfloat16), w_ref[...], preferred_element_type=jnp.float32)
    sig = jax.nn.sigmoid(pre)
    dpre = (cot_ref[...].astype(jnp.float32) * sig * (1.0 + pre * (1.0 - sig))).astype(
        jnp.bfloat16
    )
    dunit = lax.dot_general(
        dpre, w_ref[...], (((1,), (1,)), ((), ())), preferred_element_type=jnp.float32
    )
    dbag = (dunit - unit * jnp.mean(dunit * unit, axis=-1, keepdims=True)) * inv
    out_ref[...] = jnp.broadcast_to(dbag.astype(jnp.bfloat16)[None], out_ref.shape)


def dense_layer(sums, w_hidden, hidden_cot):
    return pl.pallas_call(
        dense_layer_kernel,
        out_shape=jax.ShapeDtypeStruct(sums.shape, jnp.bfloat16),
        compiler_params=pltpu.CompilerParams(vmem_limit_bytes=16 * 2**20),
        name="dense_layer",
    )(sums, w_hidden, hidden_cot)


def route_kernel(nh, proteins, block_ref, protein_ref, weight_ref, out_ref):
    nz, rows, block_rows = out_ref.shape
    pairs = block_ref.shape[1]
    per_z = rows - 8
    slots = nz * per_z
    block = block_ref[...]
    owner = block // BLK_DEV
    code = (protein_ref[...] % proteins) * BLK_DEV + block % BLK_DEV + 1

    square = (pairs, pairs)
    down = lax.broadcasted_iota(jnp.int32, square, 0)
    across = lax.broadcasted_iota(jnp.int32, square, 1)
    owner_f = owner.astype(jnp.float32)
    column = jnp.sum(jnp.where(down == across, owner_f, 0.0), axis=1, keepdims=True)
    earlier = jnp.where((column == owner_f) & (down < across), 1.0, 0.0)
    rank = jnp.sum(earlier, axis=0, keepdims=True).astype(jnp.int32)

    oz = (owner % (nz * nh)) // nh
    opl = (owner // (nz * nh)) * nh + owner % nh
    within = opl * CAP + rank
    slot = oz * per_z + within
    place = lax.broadcasted_iota(jnp.int32, (slots, pairs), 0) == slot
    send = jnp.dot(
        jnp.where(place, 1.0, 0.0).astype(jnp.bfloat16),
        weight_ref[...],
        preferred_element_type=jnp.float32,
    )
    mine = lax.broadcasted_iota(jnp.int32, (nz, pairs), 0) == oz
    lane = lax.broadcasted_iota(jnp.int32, (block_rows, pairs), 0) == within
    codes = lax.dot_general(
        jnp.where(mine, code.astype(jnp.float32), 0.0).astype(jnp.bfloat16),
        jnp.where(lane, 1.0, 0.0).astype(jnp.bfloat16),
        (((1,), (1,)), ((), ())),
        preferred_element_type=jnp.float32,
    )
    out_ref[...] = jnp.concatenate(
        [
            send.reshape(nz, per_z, block_rows),
            jnp.broadcast_to(codes[:, None, :], (nz, 8, block_rows)),
        ],
        axis=1,
    ).astype(jnp.bfloat16)


def route(pair_block, pair_protein, pair_weight, nz, nh, per_z, proteins):
    pairs, block_rows = pair_weight.shape
    return pl.pallas_call(
        functools.partial(route_kernel, nh, proteins),
        out_shape=jax.ShapeDtypeStruct((nz, per_z + 8, block_rows), jnp.bfloat16),
        compiler_params=pltpu.CompilerParams(vmem_limit_bytes=16 * 2**20),
        name="route",
    )(
        pltpu.with_memory_space_constraint(pair_block.reshape(1, pairs), pltpu.HBM),
        pltpu.with_memory_space_constraint(pair_protein.reshape(1, pairs), pltpu.HBM),
        pltpu.with_memory_space_constraint(pair_weight, pltpu.HBM),
    )


def slot_blocks(got, per_p):
    shape = (got.shape[0], per_p, got.shape[2])
    diagonal = lax.broadcasted_iota(jnp.int32, shape, 1) == lax.broadcasted_iota(
        jnp.int32, shape, 2
    )
    row = got[:, per_p : per_p + 1, :]
    return jnp.sum(jnp.where(diagonal, row, 0.0), axis=2, keepdims=True)


def fill_dense(got, per_p, dense_ref):
    groups, _, block_rows = got.shape
    block = slot_blocks(got, per_p)
    weights = got[:, :per_p, :]
    for b in range(dense_ref.shape[1] // block_rows):
        mine = jnp.where(block == b, weights, 0.0).astype(jnp.bfloat16)
        dense_ref[:, b * block_rows : (b + 1) * block_rows] = mine.reshape(
            groups * per_p, block_rows
        )


def owner_kernel(got_ref, table_ref, partial_ref, dense_ref):
    fill_dense(got_ref[...].astype(jnp.float32), partial_ref.shape[1], dense_ref)
    partial_ref[...] = (
        jnp.dot(dense_ref[...], table_ref[...], preferred_element_type=jnp.float32)
        .astype(jnp.bfloat16)
        .reshape(partial_ref.shape)
    )


def update_kernel(
    got_ref,
    grad_ref,
    accum_ref,
    table_ref,
    table_out,
    accum_out,
    dense_ref,
    sum_ref,
    new_ref,
    out_sems,
):
    groups, per_p, width = grad_ref.shape
    block_rows = got_ref.shape[2]
    blocks = table_ref.shape[0] // block_rows
    fill_dense(got_ref[...].astype(jnp.float32), per_p, dense_ref)
    sum_ref[...] = lax.dot_general(
        dense_ref[...],
        grad_ref[...].reshape(groups * per_p, width),
        (((0,), (0,)), ((), ())),
        preferred_element_type=jnp.float32,
    )
    square = (block_rows, block_rows)
    diagonal = lax.broadcasted_iota(jnp.int32, square, 0) == lax.broadcasted_iota(
        jnp.int32, square, 1
    )
    stores = []
    for b in range(blocks):
        rows = pl.ds(b * block_rows, block_rows)
        grad = sum_ref[rows, :]
        accum = jnp.sum(jnp.where(diagonal, accum_ref[b], 0.0), axis=1, keepdims=True)
        accum = accum + jnp.mean(grad * grad, axis=1, keepdims=True)
        rate = 0.3 / (jnp.sqrt(accum) + 1e-08)
        new_ref[rows, :] = (table_ref[rows, :].astype(jnp.float32) - grad * rate).astype(
            jnp.bfloat16
        )
        accum_out[b] = jnp.sum(jnp.where(diagonal, accum, 0.0), axis=0, keepdims=True)
        store = pltpu.make_async_copy(new_ref.at[rows, :], table_out.at[rows, :], out_sems.at[b])
        store.start()
        stores.append(store)
    for store in stores:
        store.wait()


def update_rows(got, grad, table, accum):
    npl, rows, block_rows = got.shape
    _, per_p, width = grad.shape
    rows_dev = table.shape[0]
    blocks = rows_dev // block_rows
    vmem = pl.BlockSpec(memory_space=pltpu.VMEM)
    anywhere = pl.BlockSpec(memory_space=pl.ANY)
    new_table, new_accum = pl.pallas_call(
        update_kernel,
        in_specs=[vmem, vmem, vmem, vmem],
        out_specs=[anywhere, vmem],
        out_shape=[
            jax.ShapeDtypeStruct(table.shape, table.dtype),
            jax.ShapeDtypeStruct((blocks, 1, block_rows), jnp.float32),
        ],
        scratch_shapes=[
            pltpu.VMEM((npl * per_p, rows_dev), jnp.bfloat16),
            pltpu.VMEM((rows_dev, width), jnp.float32),
            pltpu.VMEM((rows_dev, width), table.dtype),
            pltpu.SemaphoreType.DMA((blocks,)),
        ],
        compiler_params=pltpu.CompilerParams(vmem_limit_bytes=24 * 2**20),
        name="update_rows",
    )(got, grad, accum.reshape(blocks, 1, block_rows), table)
    return new_table, new_accum.reshape(accum.shape)


def owner_partials(got, table, per_p):
    npl, rows, block_rows = got.shape
    rows_dev, width = table.shape
    return pl.pallas_call(
        owner_kernel,
        out_shape=jax.ShapeDtypeStruct((npl, per_p, width), jnp.bfloat16),
        scratch_shapes=[pltpu.VMEM((npl * per_p, rows_dev), jnp.bfloat16)],
        compiler_params=pltpu.CompilerParams(vmem_limit_bytes=24 * 2**20),
        name="owner_partials",
    )(got, table)


def membership(codes, proteins, per_p, slots):
    nz, lanes = codes.shape
    sums = nz * proteins
    source = lax.broadcasted_iota(jnp.int32, (sums, nz), 0) // proteins
    spread = source == lax.broadcasted_iota(jnp.int32, (sums, nz), 1)
    by_row = jnp.dot(
        jnp.where(spread, 1.0, 0.0).astype(jnp.bfloat16),
        codes,
        preferred_element_type=jnp.float32,
    ).astype(jnp.bfloat16)
    slot = lax.broadcasted_iota(jnp.int32, (lanes, slots), 1)
    entry = (slot // per_p) * CAP + slot % CAP
    move = lax.broadcasted_iota(jnp.int32, (lanes, slots), 0) == entry
    code = jnp.dot(
        by_row, jnp.where(move, 1.0, 0.0).astype(jnp.bfloat16), preferred_element_type=jnp.float32
    ).astype(jnp.int32)
    row = lax.broadcasted_iota(jnp.int32, (sums, slots), 0)
    slot = lax.broadcasted_iota(jnp.int32, (sums, slots), 1)
    low = (row % proteins) * BLK_DEV
    mine = (row // proteins == (slot % per_p) // CAP) & (code > low) & (code <= low + BLK_DEV)
    return jnp.where(mine, 1.0, 0.0).astype(jnp.bfloat16)


def sum_kernel(codes_ref, got_ref, out_ref, member_ref):
    proteins = out_ref.shape[1]
    _, per_p, width = got_ref.shape
    slots = member_ref.shape[1]
    member_ref[...] = membership(codes_ref[...], proteins, per_p, slots)
    total = jnp.dot(
        member_ref[...], got_ref[...].reshape(slots, width), preferred_element_type=jnp.float32
    )
    out_ref[...] = total.reshape(out_ref.shape)


def protein_sums(codes, got, proteins):
    nz = codes.shape[0]
    npl, per_p, width = got.shape
    return pl.pallas_call(
        sum_kernel,
        out_shape=[
            jax.ShapeDtypeStruct((nz, proteins, width), jnp.float32),
            jax.ShapeDtypeStruct((nz * proteins, npl * per_p), jnp.bfloat16),
        ],
        compiler_params=pltpu.CompilerParams(vmem_limit_bytes=16 * 2**20),
        name="protein_sums",
    )(codes, got)


def select_kernel(member_ref, every_ref, out_ref):
    nz, proteins, width = every_ref.shape
    picked = lax.dot_general(
        member_ref[...],
        every_ref[...].astype(jnp.float32).reshape(nz * proteins, width).astype(jnp.bfloat16),
        (((0,), (0,)), ((), ())),
        preferred_element_type=jnp.float32,
    )
    out_ref[...] = picked.astype(jnp.bfloat16).reshape(out_ref.shape)


def select_grads(member, every, npl):
    slots = member.shape[1]
    width = every.shape[2]
    return pl.pallas_call(
        select_kernel,
        out_shape=jax.ShapeDtypeStruct((npl, slots // npl, width), jnp.bfloat16),
        compiler_params=pltpu.CompilerParams(vmem_limit_bytes=16 * 2**20),
        name="select_grads",
    )(member, every)


def exchange(x, axes):
    return lax.all_to_all(x, axes, split_axis=0, concat_axis=0, tiled=True)


def per_device(table, accum, pair_block, pair_protein, pair_weight, w_hidden, hidden_cot):
    nz = lax.axis_size("z")
    npl = lax.axis_size(PLANE)
    block_rows = pair_weight.shape[1]
    proteins, width = hidden_cot.shape
    per_z = npl * CAP
    per_p = nz * CAP

    first = route(
        pair_block, pair_protein, pair_weight, nz, lax.axis_size("xh"), per_z, proteins
    )
    first = exchange(first, "z")

    weights = first[:, :per_z].reshape(nz, npl, CAP, block_rows).transpose(1, 0, 2, 3)
    codes = lax.optimization_barrier(first[:, per_z, :per_z])
    code = codes.astype(jnp.int32).reshape(nz, npl, CAP).transpose(1, 0, 2)
    block = ((code - 1) & (BLK_DEV - 1)).astype(jnp.bfloat16).reshape(npl, 1, per_p)
    block = jnp.pad(block, ((0, 0), (0, 7), (0, block_rows - per_p)))
    second = exchange(
        jnp.concatenate([weights.reshape(npl, per_p, block_rows), block], axis=1), PLANE
    )
    partial_value = owner_partials(second, table, per_p)

    sums, member = protein_sums(codes, exchange(partial_value, PLANE), proteins)
    dbag = dense_layer(exchange(sums, "z"), w_hidden, hidden_cot)

    every = exchange(dbag, "z")
    grad = exchange(select_grads(member, every, npl), PLANE)
    return update_rows(second, grad, table, accum)


def solution(mesh):
    split = Mesh(mesh.devices.reshape(SIZES), AXES)
    in_specs = (
        P(AXES, None),
        P(AXES),
        P(AXES),
        P(AXES),
        P(AXES, None),
        P(),
        P(AXES, None),
    )
    out_specs = (P(AXES, None), P(AXES))
    return jax.shard_map(
        per_device, mesh=split, in_specs=in_specs, out_specs=out_specs, check_vma=False
    )
```

```python
import functools

import jax
import jax.numpy as jnp
from jax import lax
from jax.experimental import pallas as pl
from jax.experimental.pallas import tpu as pltpu
from jax.sharding import Mesh
from jax.sharding import PartitionSpec as P

CAP = 2
BLK_DEV = 4
AXES = ("xl", "y", "c", "z", "zl", "xh")
SIZES = (2, 4, 2, 8, 2, 2)
LINE = ("zl", "z")
PLANE = ("xl", "y", "c", "xh")
GROUP = ("xl", "y", "c", "xh", "zl")


def dense_layer_kernel(sums_ref, w_ref, cot_ref, out_ref):
    nz = sums_ref.shape[0]
    bag = sums_ref[0]
    for z in range(1, nz):
        bag = bag + sums_ref[z]
    inv = lax.rsqrt(jnp.mean(bag * bag, axis=-1, keepdims=True) + 1e-06)
    unit = bag * inv
    pre = jnp.dot(unit.astype(jnp.bfloat16), w_ref[...], preferred_element_type=jnp.float32)
    sig = jax.nn.sigmoid(pre)
    dpre = (cot_ref[...].astype(jnp.float32) * sig * (1.0 + pre * (1.0 - sig))).astype(
        jnp.bfloat16
    )
    dunit = lax.dot_general(
        dpre, w_ref[...], (((1,), (1,)), ((), ())), preferred_element_type=jnp.float32
    )
    dbag = (dunit - unit * jnp.mean(dunit * unit, axis=-1, keepdims=True)) * inv
    lanes = out_ref.shape[2]
    rows = [dbag[:, j : j + lanes] for j in range(0, dbag.shape[1], lanes)]
    message = jnp.concatenate(rows, axis=0).astype(jnp.bfloat16)
    out_ref[...] = jnp.broadcast_to(message[None], out_ref.shape)


def dense_layer(sums, w_hidden, hidden_cot):
    nz, proteins, width = sums.shape
    return pl.pallas_call(
        dense_layer_kernel,
        out_shape=jax.ShapeDtypeStruct((nz, proteins * width // 128, 128), jnp.bfloat16),
        compiler_params=pltpu.CompilerParams(vmem_limit_bytes=16 * 2**20),
        name="dense_layer",
    )(sums, w_hidden, hidden_cot)


def route_kernel(
    nl, nh, proteins, block_in, protein_in, weight_in, out_ref, block_ref, protein_ref, weight_ref, sems
):
    copies = [
        pltpu.make_async_copy(source, target, sems.at[i])
        for i, (source, target) in enumerate(
            [(block_in, block_ref), (protein_in, protein_ref), (weight_in, weight_ref)]
        )
    ]
    for copy in copies:
        copy.start()
    for copy in copies:
        copy.wait()
    line, rows, block_rows = out_ref.shape
    pairs = block_ref.shape[1]
    per_z = rows - 8
    slots = line * per_z
    block = block_ref[...]
    owner = block // BLK_DEV
    code = (protein_ref[...] % proteins) * BLK_DEV + block % BLK_DEV + 1

    square = (pairs, pairs)
    down = lax.broadcasted_iota(jnp.int32, square, 0)
    across = lax.broadcasted_iota(jnp.int32, square, 1)
    owner_f = owner.astype(jnp.float32)
    column = jnp.sum(jnp.where(down == across, owner_f, 0.0), axis=1, keepdims=True)
    earlier = jnp.where((column == owner_f) & (down < across), 1.0, 0.0)
    rank = jnp.sum(earlier, axis=0, keepdims=True).astype(jnp.int32)

    n_dp = line * nh
    nz = line // nl
    along = (owner % n_dp) // nh
    z, zl = along // nl, along % nl
    plane = (owner // n_dp) * nh + owner % nh
    place = lax.broadcasted_iota(jnp.int32, (slots, pairs), 0) == (
        (zl * nz + z) * per_z + plane * CAP + rank
    )
    send = jnp.dot(
        jnp.where(place, 1.0, 0.0).astype(jnp.bfloat16),
        weight_ref[...],
        preferred_element_type=jnp.float32,
    )

    def code_rows(row, count, lane):
        mine = lax.broadcasted_iota(jnp.int32, (count, pairs), 0) == row
        here = lax.broadcasted_iota(jnp.int32, (block_rows, pairs), 0) == lane
        return lax.dot_general(
            jnp.where(mine, code.astype(jnp.float32), 0.0).astype(jnp.bfloat16),
            jnp.where(here, 1.0, 0.0).astype(jnp.bfloat16),
            (((1,), (1,)), ((), ())),
            preferred_element_type=jnp.float32,
        )

    own = code_rows(zl * nz + z, line, plane * CAP + rank)
    both = code_rows(z, nz, (plane * nl + zl) * CAP + rank)
    both = jnp.concatenate([both] * nl, axis=0)
    row = lax.broadcasted_iota(jnp.int32, (line, 8, block_rows), 1)
    out_ref[...] = jnp.concatenate(
        [
            send.reshape(line, per_z, block_rows),
            jnp.where(row == 0, own[:, None, :], both[:, None, :]),
        ],
        axis=1,
    ).astype(jnp.bfloat16)


def route(pair_block, pair_protein, pair_weight, line, nl, nh, per_z, proteins):
    pairs, block_rows = pair_weight.shape
    return pl.pallas_call(
        functools.partial(route_kernel, nl, nh, proteins),
        in_specs=[pl.BlockSpec(memory_space=pl.ANY)] * 3,
        out_shape=jax.ShapeDtypeStruct((line, per_z + 8, block_rows), jnp.bfloat16),
        scratch_shapes=[
            pltpu.VMEM((1, pairs), jnp.int32),
            pltpu.VMEM((1, pairs), jnp.int32),
            pltpu.VMEM((pairs, block_rows), jnp.bfloat16),
            pltpu.SemaphoreType.DMA((3,)),
        ],
        compiler_params=pltpu.CompilerParams(vmem_limit_bytes=16 * 2**20),
        name="route",
    )(
        pltpu.with_memory_space_constraint(pair_block.reshape(1, pairs), pltpu.HBM),
        pltpu.with_memory_space_constraint(pair_protein.reshape(1, pairs), pltpu.HBM),
        pltpu.with_memory_space_constraint(pair_weight, pltpu.HBM),
    )


def slot_blocks(got, per_p):
    shape = (got.shape[0], per_p, got.shape[2])
    diagonal = lax.broadcasted_iota(jnp.int32, shape, 1) == lax.broadcasted_iota(
        jnp.int32, shape, 2
    )
    row = got[:, per_p : per_p + 1, :]
    return jnp.sum(jnp.where(diagonal, row, 0.0), axis=2, keepdims=True)


def fill_dense(got, per_p, dense_ref):
    groups, _, block_rows = got.shape
    block = slot_blocks(got, per_p)
    weights = got[:, :per_p, :]
    for b in range(dense_ref.shape[1] // block_rows):
        mine = jnp.where(block == b, weights, 0.0).astype(jnp.bfloat16)
        dense_ref[:, b * block_rows : (b + 1) * block_rows] = mine.reshape(
            groups * per_p, block_rows
        )


def owner_kernel(got_ref, table_ref, partial_ref, dense_ref):
    fill_dense(got_ref[...].astype(jnp.float32), got_ref.shape[1] - 8, dense_ref)
    partial_ref[...] = (
        jnp.dot(dense_ref[...], table_ref[...], preferred_element_type=jnp.float32)
        .astype(jnp.bfloat16)
        .reshape(partial_ref.shape)
    )


def update_kernel(
    got_ref,
    grad_ref,
    accum_ref,
    table_ref,
    table_out,
    accum_out,
    dense_ref,
    sum_ref,
):
    slots = grad_ref.shape[0] * grad_ref.shape[1]
    width = grad_ref.shape[2]
    block_rows = got_ref.shape[2]
    blocks = table_ref.shape[0] // block_rows
    fill_dense(got_ref[...].astype(jnp.float32), got_ref.shape[1] - 8, dense_ref)
    sum_ref[...] = lax.dot_general(
        dense_ref[...],
        grad_ref[...].reshape(slots, width),
        (((0,), (0,)), ((), ())),
        preferred_element_type=jnp.float32,
    )
    square = (block_rows, block_rows)
    diagonal = lax.broadcasted_iota(jnp.int32, square, 0) == lax.broadcasted_iota(
        jnp.int32, square, 1
    )
    for b in range(blocks):
        rows = slice(b * block_rows, (b + 1) * block_rows)
        grad = sum_ref[rows, :]
        accum = jnp.sum(jnp.where(diagonal, accum_ref[b], 0.0), axis=1, keepdims=True)
        accum = accum + jnp.mean(grad * grad, axis=1, keepdims=True)
        rate = 0.3 / (jnp.sqrt(accum) + 1e-08)
        table_out[rows, :] = (table_ref[rows, :].astype(jnp.float32) - grad * rate).astype(
            jnp.bfloat16
        )
        accum_out[b] = jnp.sum(jnp.where(diagonal, accum, 0.0), axis=0, keepdims=True)


def update_rows(got, grad, table, accum):
    block_rows = got.shape[2]
    slots, width = grad.shape[0] * grad.shape[1], grad.shape[2]
    rows_dev = table.shape[0]
    blocks = rows_dev // block_rows
    new_table, new_accum = pl.pallas_call(
        update_kernel,
        out_shape=[
            jax.ShapeDtypeStruct(table.shape, table.dtype),
            jax.ShapeDtypeStruct((blocks, 1, block_rows), jnp.float32),
        ],
        scratch_shapes=[
            pltpu.VMEM((slots, rows_dev), jnp.bfloat16),
            pltpu.VMEM((rows_dev, width), jnp.float32),
        ],
        compiler_params=pltpu.CompilerParams(vmem_limit_bytes=24 * 2**20),
        name="update_rows",
    )(got, grad, accum.reshape(blocks, 1, block_rows), table)
    return new_table, new_accum.reshape(accum.shape)


def owner_partials(got, table, targets):
    slots = got.shape[0] * (got.shape[1] - 8)
    rows_dev, width = table.shape
    return pl.pallas_call(
        owner_kernel,
        out_shape=jax.ShapeDtypeStruct((targets, slots // targets, width), jnp.bfloat16),
        scratch_shapes=[pltpu.VMEM((slots, rows_dev), jnp.bfloat16)],
        compiler_params=pltpu.CompilerParams(vmem_limit_bytes=24 * 2**20),
        name="owner_partials",
    )(got, table)


def membership(codes, first_row, sums, proteins, per_p, slots):
    rows, lanes = codes.shape
    source = lax.broadcasted_iota(jnp.int32, (sums, rows), 0) // proteins + first_row
    spread = source == lax.broadcasted_iota(jnp.int32, (sums, rows), 1)
    by_row = jnp.dot(
        jnp.where(spread, 1.0, 0.0).astype(jnp.bfloat16),
        codes,
        preferred_element_type=jnp.float32,
    ).astype(jnp.bfloat16)
    slot = lax.broadcasted_iota(jnp.int32, (lanes, slots), 1)
    entry = (slot // per_p) * CAP + slot % CAP
    move = lax.broadcasted_iota(jnp.int32, (lanes, slots), 0) == entry
    code = jnp.dot(
        by_row, jnp.where(move, 1.0, 0.0).astype(jnp.bfloat16), preferred_element_type=jnp.float32
    ).astype(jnp.int32)
    row = lax.broadcasted_iota(jnp.int32, (sums, slots), 0)
    slot = lax.broadcasted_iota(jnp.int32, (sums, slots), 1)
    low = (row % proteins) * BLK_DEV
    mine = (row // proteins == (slot % per_p) // CAP) & (code > low) & (code <= low + BLK_DEV)
    return jnp.where(mine, 1.0, 0.0).astype(jnp.bfloat16)


def sum_kernel(codes_ref, got_ref, out_ref, member_ref):
    nz, proteins, _ = out_ref.shape
    _, per_p, width = got_ref.shape
    sums, slots = member_ref.shape
    codes = codes_ref[...].astype(jnp.float32)[:, 1, :].astype(jnp.bfloat16)
    member_ref[...] = membership(
        codes, lax.axis_index("zl") * nz, sums, proteins, per_p, slots
    )
    total = jnp.dot(
        member_ref[...], got_ref[...].reshape(slots, width), preferred_element_type=jnp.float32
    )
    out_ref[...] = total.reshape(out_ref.shape)


def protein_sums(codes, got, nz, proteins):
    npl, per_p, width = got.shape
    return pl.pallas_call(
        sum_kernel,
        out_shape=[
            jax.ShapeDtypeStruct((nz, proteins, width), jnp.float32),
            jax.ShapeDtypeStruct((nz * proteins, npl * per_p), jnp.bfloat16),
        ],
        compiler_params=pltpu.CompilerParams(vmem_limit_bytes=16 * 2**20),
        name="protein_sums",
    )(codes, got)


def select_kernel(member_ref, every_ref, out_ref):
    nz, rows, lanes = every_ref.shape
    width = out_ref.shape[2]
    proteins = rows * lanes // width
    every = every_ref[...].astype(jnp.float32)
    every = jnp.concatenate(
        [
            every[:, j : j + proteins, :].reshape(nz * proteins, lanes)
            for j in range(0, rows, proteins)
        ],
        axis=1,
    )
    picked = lax.dot_general(
        member_ref[...],
        every.astype(jnp.bfloat16),
        (((0,), (0,)), ((), ())),
        preferred_element_type=jnp.float32,
    )
    out_ref[...] = picked.astype(jnp.bfloat16).reshape(out_ref.shape)


def select_grads(member, every, npl, width):
    slots = member.shape[1]
    return pl.pallas_call(
        select_kernel,
        out_shape=jax.ShapeDtypeStruct((npl, slots // npl, width), jnp.bfloat16),
        compiler_params=pltpu.CompilerParams(vmem_limit_bytes=16 * 2**20),
        name="select_grads",
    )(member, every)


def exchange(x, axes):
    return lax.all_to_all(x, axes, split_axis=0, concat_axis=0, tiled=True)


def per_device(table, accum, pair_block, pair_protein, pair_weight, w_hidden, hidden_cot):
    nz, nl, nh = lax.axis_size("z"), lax.axis_size("zl"), lax.axis_size("xh")
    line, plane, group = nz * nl, lax.axis_size(PLANE), lax.axis_size(GROUP)
    block_rows = pair_weight.shape[1]
    proteins, width = hidden_cot.shape
    per_z = plane * CAP
    per_p = line * CAP

    first = route(pair_block, pair_protein, pair_weight, line, nl, nh, per_z, proteins)
    first = exchange(first, LINE)

    weights = first[:, :per_z].reshape(line, plane, CAP, block_rows).transpose(1, 0, 2, 3)
    codes = lax.optimization_barrier(first[:, per_z:])
    code = codes[:, 0, :per_z].astype(jnp.int32).reshape(line, plane, CAP).transpose(1, 0, 2)
    block = ((code - 1) & (BLK_DEV - 1)).astype(jnp.bfloat16).reshape(plane, 1, per_p)
    block = jnp.pad(block, ((0, 0), (0, 7), (0, block_rows - per_p)))
    second = exchange(
        jnp.concatenate([weights.reshape(plane, per_p, block_rows), block], axis=1), PLANE
    )
    partial_value = owner_partials(second, table, group)

    sums, member = protein_sums(codes, exchange(partial_value, GROUP), nz, proteins)
    dbag = dense_layer(exchange(sums, "z"), w_hidden, hidden_cot)

    every = exchange(dbag, "z")
    grad = exchange(select_grads(member, every, group, width), GROUP)
    return update_rows(second, grad, table, accum)


def solution(mesh):
    split = Mesh(mesh.devices.reshape(SIZES), AXES)
    in_specs = (
        P(AXES, None),
        P(AXES),
        P(AXES),
        P(AXES),
        P(AXES, None),
        P(),
        P(AXES, None),
    )
    out_specs = (P(AXES, None), P(AXES))
    return jax.shard_map(
        per_device, mesh=split, in_specs=in_specs, out_specs=out_specs, check_vma=False
    )
```

```python
import functools

import jax
import jax.numpy as jnp
from jax import lax
from jax.experimental import pallas as pl
from jax.experimental.pallas import tpu as pltpu
from jax.sharding import Mesh
from jax.sharding import PartitionSpec as P

CAP = 2
BLK_DEV = 4
AXES = ("xl", "y", "c", "z", "zl", "xh")
SIZES = (2, 4, 2, 8, 2, 2)
LINE = ("zl", "z")
PLANE = ("xl", "y", "c", "xh")
GROUP = ("xl", "y", "c", "xh", "zl")


def dense_layer_kernel(sums_ref, w_ref, cot_ref, out_ref):
    nz = sums_ref.shape[0]
    bag = sums_ref[0]
    for z in range(1, nz):
        bag = bag + sums_ref[z]
    inv = lax.rsqrt(jnp.mean(bag * bag, axis=-1, keepdims=True) + 1e-06)
    unit = bag * inv
    pre = jnp.dot(unit.astype(jnp.bfloat16), w_ref[...], preferred_element_type=jnp.float32)
    sig = jax.nn.sigmoid(pre)
    dpre = (cot_ref[...].astype(jnp.float32) * sig * (1.0 + pre * (1.0 - sig))).astype(
        jnp.bfloat16
    )
    dunit = lax.dot_general(
        dpre, w_ref[...], (((1,), (1,)), ((), ())), preferred_element_type=jnp.float32
    )
    dbag = (dunit - unit * jnp.mean(dunit * unit, axis=-1, keepdims=True)) * inv
    lanes = out_ref.shape[2]
    rows = [dbag[:, j : j + lanes] for j in range(0, dbag.shape[1], lanes)]
    message = jnp.concatenate(rows, axis=0).astype(jnp.bfloat16)
    out_ref[...] = jnp.broadcast_to(message[None], out_ref.shape)


def dense_layer(sums, w_hidden, hidden_cot):
    nz, proteins, width = sums.shape
    return pl.pallas_call(
        dense_layer_kernel,
        out_shape=jax.ShapeDtypeStruct((nz, proteins * width // 128, 128), jnp.bfloat16),
        compiler_params=pltpu.CompilerParams(vmem_limit_bytes=16 * 2**20),
        name="dense_layer",
    )(sums, w_hidden, hidden_cot)


def route_kernel(
    nl, nh, proteins, block_in, protein_in, weight_in, out_ref, block_ref, protein_ref, weight_ref, sems
):
    copies = [
        pltpu.make_async_copy(source, target, sems.at[i])
        for i, (source, target) in enumerate(
            [(block_in, block_ref), (protein_in, protein_ref), (weight_in, weight_ref)]
        )
    ]
    for copy in copies:
        copy.start()
    for copy in copies:
        copy.wait()
    line, rows, block_rows = out_ref.shape
    pairs = block_ref.shape[1]
    per_z = rows - 8
    slots = line * per_z
    block = block_ref[...]
    owner = block // BLK_DEV
    code = (protein_ref[...] % proteins) * BLK_DEV + block % BLK_DEV + 1

    square = (pairs, pairs)
    down = lax.broadcasted_iota(jnp.int32, square, 0)
    across = lax.broadcasted_iota(jnp.int32, square, 1)
    owner_f = owner.astype(jnp.float32)
    column = jnp.sum(jnp.where(down == across, owner_f, 0.0), axis=1, keepdims=True)
    earlier = jnp.where((column == owner_f) & (down < across), 1.0, 0.0)
    rank = jnp.sum(earlier, axis=0, keepdims=True).astype(jnp.int32)

    n_dp = line * nh
    nz = line // nl
    along = (owner % n_dp) // nh
    z, zl = along // nl, along % nl
    plane = (owner // n_dp) * nh + owner % nh
    place = lax.broadcasted_iota(jnp.int32, (slots, pairs), 0) == (
        (zl * nz + z) * per_z + plane * CAP + rank
    )
    send = jnp.dot(
        jnp.where(place, 1.0, 0.0).astype(jnp.bfloat16),
        weight_ref[...],
        preferred_element_type=jnp.float32,
    )

    def code_rows(row, count, lane):
        mine = lax.broadcasted_iota(jnp.int32, (count, pairs), 0) == row
        here = lax.broadcasted_iota(jnp.int32, (block_rows, pairs), 0) == lane
        return lax.dot_general(
            jnp.where(mine, code.astype(jnp.float32), 0.0).astype(jnp.bfloat16),
            jnp.where(here, 1.0, 0.0).astype(jnp.bfloat16),
            (((1,), (1,)), ((), ())),
            preferred_element_type=jnp.float32,
        )

    own = code_rows(zl * nz + z, line, plane * CAP + rank)
    both = code_rows(z, nz, (plane * nl + zl) * CAP + rank)
    both = jnp.concatenate([both] * nl, axis=0)
    row = lax.broadcasted_iota(jnp.int32, (line, 8, block_rows), 1)
    out_ref[...] = jnp.concatenate(
        [
            send.reshape(line, per_z, block_rows),
            jnp.where(row == 0, own[:, None, :], both[:, None, :]),
        ],
        axis=1,
    ).astype(jnp.bfloat16)


def route(pair_block, pair_protein, pair_weight, line, nl, nh, per_z, proteins):
    pairs, block_rows = pair_weight.shape
    return pl.pallas_call(
        functools.partial(route_kernel, nl, nh, proteins),
        in_specs=[pl.BlockSpec(memory_space=pl.ANY)] * 3,
        out_shape=jax.ShapeDtypeStruct((line, per_z + 8, block_rows), jnp.bfloat16),
        scratch_shapes=[
            pltpu.VMEM((1, pairs), jnp.int32),
            pltpu.VMEM((1, pairs), jnp.int32),
            pltpu.VMEM((pairs, block_rows), jnp.bfloat16),
            pltpu.SemaphoreType.DMA((3,)),
        ],
        compiler_params=pltpu.CompilerParams(vmem_limit_bytes=16 * 2**20),
        name="route",
    )(
        pltpu.with_memory_space_constraint(pair_block.reshape(1, pairs), pltpu.HBM),
        pltpu.with_memory_space_constraint(pair_protein.reshape(1, pairs), pltpu.HBM),
        pltpu.with_memory_space_constraint(pair_weight, pltpu.HBM),
    )


def slot_blocks(got, per_p):
    shape = (got.shape[0], per_p, got.shape[2])
    diagonal = lax.broadcasted_iota(jnp.int32, shape, 1) == lax.broadcasted_iota(
        jnp.int32, shape, 2
    )
    row = got[:, per_p : per_p + 1, :]
    return jnp.sum(jnp.where(diagonal, row, 0.0), axis=2, keepdims=True)


def fill_dense(got, per_p, dense_ref):
    groups, _, block_rows = got.shape
    block = slot_blocks(got, per_p)
    weights = got[:, :per_p, :]
    for b in range(dense_ref.shape[1] // block_rows):
        mine = jnp.where(block == b, weights, 0.0).astype(jnp.bfloat16)
        dense_ref[:, b * block_rows : (b + 1) * block_rows] = mine.reshape(
            groups * per_p, block_rows
        )


def owner_kernel(got_ref, table_ref, partial_ref, dense_ref):
    fill_dense(got_ref[...].astype(jnp.float32), got_ref.shape[1] - 8, dense_ref)
    partial_ref[...] = (
        jnp.dot(dense_ref[...], table_ref[...], preferred_element_type=jnp.float32)
        .astype(jnp.bfloat16)
        .reshape(partial_ref.shape)
    )


def update_kernel(dense_ref, grad_ref, accum_ref, table_ref, table_out, accum_out, sum_ref):
    slots = dense_ref.shape[0]
    block_rows = accum_ref.shape[2]
    sum_ref[...] = lax.dot_general(
        dense_ref[...],
        grad_ref[...].reshape(slots, grad_ref.shape[2]),
        (((0,), (0,)), ((), ())),
        preferred_element_type=jnp.float32,
    )
    square = (block_rows, block_rows)
    diagonal = lax.broadcasted_iota(jnp.int32, square, 0) == lax.broadcasted_iota(
        jnp.int32, square, 1
    )
    for b in range(accum_ref.shape[0]):
        rows = slice(b * block_rows, (b + 1) * block_rows)
        grad = sum_ref[rows, :]
        accum = jnp.sum(jnp.where(diagonal, accum_ref[b], 0.0), axis=1, keepdims=True)
        accum = accum + jnp.mean(grad * grad, axis=1, keepdims=True)
        rate = 0.3 / (jnp.sqrt(accum) + 1e-08)
        table_out[rows, :] = (table_ref[rows, :].astype(jnp.float32) - grad * rate).astype(
            jnp.bfloat16
        )
        accum_out[b] = jnp.sum(jnp.where(diagonal, accum, 0.0), axis=0, keepdims=True)


def update_rows(dense, grad, table, accum, block_rows):
    rows_dev, width = table.shape
    blocks = rows_dev // block_rows
    new_table, new_accum = pl.pallas_call(
        update_kernel,
        out_shape=[
            jax.ShapeDtypeStruct(table.shape, table.dtype),
            jax.ShapeDtypeStruct((blocks, 1, block_rows), jnp.float32),
        ],
        scratch_shapes=[pltpu.VMEM((rows_dev, width), jnp.float32)],
        compiler_params=pltpu.CompilerParams(vmem_limit_bytes=24 * 2**20),
        name="update_rows",
    )(dense, grad, accum.reshape(blocks, 1, block_rows), table)
    return new_table, new_accum.reshape(accum.shape)


def owner_partials(got, table, targets):
    slots = got.shape[0] * (got.shape[1] - 8)
    rows_dev, width = table.shape
    return pl.pallas_call(
        owner_kernel,
        out_shape=[
            jax.ShapeDtypeStruct((targets, slots // targets, width), jnp.bfloat16),
            jax.ShapeDtypeStruct((slots, rows_dev), jnp.bfloat16),
        ],
        compiler_params=pltpu.CompilerParams(vmem_limit_bytes=24 * 2**20),
        name="owner_partials",
    )(got, table)


def membership(codes, first_row, sums, proteins, per_p, slots):
    rows, lanes = codes.shape
    source = lax.broadcasted_iota(jnp.int32, (sums, rows), 0) // proteins + first_row
    spread = source == lax.broadcasted_iota(jnp.int32, (sums, rows), 1)
    by_row = jnp.dot(
        jnp.where(spread, 1.0, 0.0).astype(jnp.bfloat16),
        codes,
        preferred_element_type=jnp.float32,
    ).astype(jnp.bfloat16)
    slot = lax.broadcasted_iota(jnp.int32, (lanes, slots), 1)
    entry = (slot // per_p) * CAP + slot % CAP
    move = lax.broadcasted_iota(jnp.int32, (lanes, slots), 0) == entry
    code = jnp.dot(
        by_row, jnp.where(move, 1.0, 0.0).astype(jnp.bfloat16), preferred_element_type=jnp.float32
    ).astype(jnp.int32)
    row = lax.broadcasted_iota(jnp.int32, (sums, slots), 0)
    slot = lax.broadcasted_iota(jnp.int32, (sums, slots), 1)
    low = (row % proteins) * BLK_DEV
    mine = (row // proteins == (slot % per_p) // CAP) & (code > low) & (code <= low + BLK_DEV)
    return jnp.where(mine, 1.0, 0.0).astype(jnp.bfloat16)


def sum_kernel(codes_ref, got_ref, out_ref, member_ref):
    nz, proteins, _ = out_ref.shape
    _, per_p, width = got_ref.shape
    sums, slots = member_ref.shape
    codes = codes_ref[...].astype(jnp.float32)[:, 1, :].astype(jnp.bfloat16)
    member_ref[...] = membership(
        codes, lax.axis_index("zl") * nz, sums, proteins, per_p, slots
    )
    total = jnp.dot(
        member_ref[...], got_ref[...].reshape(slots, width), preferred_element_type=jnp.float32
    )
    out_ref[...] = total.reshape(out_ref.shape)


def protein_sums(codes, got, nz, proteins):
    npl, per_p, width = got.shape
    return pl.pallas_call(
        sum_kernel,
        out_shape=[
            jax.ShapeDtypeStruct((nz, proteins, width), jnp.float32),
            jax.ShapeDtypeStruct((nz * proteins, npl * per_p), jnp.bfloat16),
        ],
        compiler_params=pltpu.CompilerParams(vmem_limit_bytes=16 * 2**20),
        name="protein_sums",
    )(codes, got)


def select_kernel(member_ref, every_ref, out_ref):
    nz, rows, lanes = every_ref.shape
    width = out_ref.shape[2]
    proteins = rows * lanes // width
    every = every_ref[...].astype(jnp.float32)
    every = jnp.concatenate(
        [
            every[:, j : j + proteins, :].reshape(nz * proteins, lanes)
            for j in range(0, rows, proteins)
        ],
        axis=1,
    )
    picked = lax.dot_general(
        member_ref[...],
        every.astype(jnp.bfloat16),
        (((0,), (0,)), ((), ())),
        preferred_element_type=jnp.float32,
    )
    out_ref[...] = picked.astype(jnp.bfloat16).reshape(out_ref.shape)


def select_grads(member, every, npl, width):
    slots = member.shape[1]
    return pl.pallas_call(
        select_kernel,
        out_shape=jax.ShapeDtypeStruct((npl, slots // npl, width), jnp.bfloat16),
        compiler_params=pltpu.CompilerParams(vmem_limit_bytes=16 * 2**20),
        name="select_grads",
    )(member, every)


def exchange(x, axes):
    return lax.all_to_all(x, axes, split_axis=0, concat_axis=0, tiled=True)


def per_device(table, accum, pair_block, pair_protein, pair_weight, w_hidden, hidden_cot):
    nz, nl, nh = lax.axis_size("z"), lax.axis_size("zl"), lax.axis_size("xh")
    line, plane, group = nz * nl, lax.axis_size(PLANE), lax.axis_size(GROUP)
    block_rows = pair_weight.shape[1]
    proteins, width = hidden_cot.shape
    per_z = plane * CAP
    per_p = line * CAP

    first = route(pair_block, pair_protein, pair_weight, line, nl, nh, per_z, proteins)
    first = exchange(first, LINE)

    weights = first[:, :per_z].reshape(line, plane, CAP, block_rows).transpose(1, 0, 2, 3)
    codes = lax.optimization_barrier(first[:, per_z:])
    code = codes[:, 0, :per_z].astype(jnp.int32).reshape(line, plane, CAP).transpose(1, 0, 2)
    block = ((code - 1) & (BLK_DEV - 1)).astype(jnp.bfloat16).reshape(plane, 1, per_p)
    block = jnp.pad(block, ((0, 0), (0, 7), (0, block_rows - per_p)))
    second = exchange(
        jnp.concatenate([weights.reshape(plane, per_p, block_rows), block], axis=1), PLANE
    )
    partial_value, dense = owner_partials(second, table, group)

    sums, member = protein_sums(codes, exchange(partial_value, GROUP), nz, proteins)
    dbag = dense_layer(exchange(sums, "z"), w_hidden, hidden_cot)

    every = exchange(dbag, "z")
    grad = exchange(select_grads(member, every, group, width), GROUP)
    return update_rows(dense, grad, table, accum, block_rows)


def solution(mesh):
    split = Mesh(mesh.devices.reshape(SIZES), AXES)
    in_specs = (
        P(AXES, None),
        P(AXES),
        P(AXES),
        P(AXES),
        P(AXES, None),
        P(),
        P(AXES, None),
    )
    out_specs = (P(AXES, None), P(AXES))
    return jax.shard_map(
        per_device, mesh=split, in_specs=in_specs, out_specs=out_specs, check_vma=False
    )
```

```python
import functools

import jax
import jax.numpy as jnp
from jax import lax
from jax.experimental import pallas as pl
from jax.experimental.pallas import tpu as pltpu
from jax.sharding import Mesh
from jax.sharding import PartitionSpec as P

CAP = 2
BLK_DEV = 4
AXES = ("xl", "y", "c", "z", "zl", "xh")
SIZES = (2, 4, 2, 8, 2, 2)
LINE = ("zl", "z")
PLANE = ("xl", "y", "c", "xh")
GROUP = ("xl", "y", "c", "xh", "zl")


def dense_layer_kernel(sums_ref, w_ref, cot_ref, out_ref):
    nz = sums_ref.shape[0]
    bag = sums_ref[0]
    for z in range(1, nz):
        bag = bag + sums_ref[z]
    inv = lax.rsqrt(jnp.mean(bag * bag, axis=-1, keepdims=True) + 1e-06)
    unit = bag * inv
    pre = jnp.dot(unit.astype(jnp.bfloat16), w_ref[...], preferred_element_type=jnp.float32)
    sig = jax.nn.sigmoid(pre)
    dpre = (cot_ref[...].astype(jnp.float32) * sig * (1.0 + pre * (1.0 - sig))).astype(
        jnp.bfloat16
    )
    dunit = lax.dot_general(
        dpre, w_ref[...], (((1,), (1,)), ((), ())), preferred_element_type=jnp.float32
    )
    dbag = (dunit - unit * jnp.mean(dunit * unit, axis=-1, keepdims=True)) * inv
    lanes = out_ref.shape[2]
    rows = [dbag[:, j : j + lanes] for j in range(0, dbag.shape[1], lanes)]
    message = jnp.concatenate(rows, axis=0).astype(jnp.bfloat16)
    out_ref[...] = jnp.broadcast_to(message[None], out_ref.shape)


def dense_layer(sums, w_hidden, hidden_cot):
    nz, proteins, width = sums.shape
    return pl.pallas_call(
        dense_layer_kernel,
        out_shape=jax.ShapeDtypeStruct((nz, proteins * width // 128, 128), jnp.bfloat16),
        compiler_params=pltpu.CompilerParams(vmem_limit_bytes=16 * 2**20),
        name="dense_layer",
    )(sums, w_hidden, hidden_cot)


def route_kernel(
    nl, nh, proteins, block_in, protein_in, weight_in, out_ref, block_ref, protein_ref, weight_ref, sems
):
    copies = [
        pltpu.make_async_copy(source, target, sems.at[i])
        for i, (source, target) in enumerate(
            [(block_in, block_ref), (protein_in, protein_ref), (weight_in, weight_ref)]
        )
    ]
    for copy in copies:
        copy.start()
    for copy in copies:
        copy.wait()
    line, groups, _, block_rows = out_ref.shape
    pairs = block_ref.shape[1]
    per_z = (groups - 1) * CAP
    slots = line * per_z
    block = block_ref[...]
    owner = block // BLK_DEV
    code = (protein_ref[...] % proteins) * BLK_DEV + block % BLK_DEV + 1

    square = (pairs, pairs)
    down = lax.broadcasted_iota(jnp.int32, square, 0)
    across = lax.broadcasted_iota(jnp.int32, square, 1)
    owner_f = owner.astype(jnp.float32)
    column = jnp.sum(jnp.where(down == across, owner_f, 0.0), axis=1, keepdims=True)
    earlier = jnp.where((column == owner_f) & (down < across), 1.0, 0.0)
    rank = jnp.sum(earlier, axis=0, keepdims=True).astype(jnp.int32)

    n_dp = line * nh
    nz = line // nl
    along = (owner % n_dp) // nh
    z, zl = along // nl, along % nl
    plane = (owner // n_dp) * nh + owner % nh
    place = lax.broadcasted_iota(jnp.int32, (slots, pairs), 0) == (
        (zl * nz + z) * per_z + plane * CAP + rank
    )
    send = jnp.dot(
        jnp.where(place, 1.0, 0.0).astype(jnp.bfloat16),
        weight_ref[...],
        preferred_element_type=jnp.float32,
    )

    def code_rows(row, count, lane):
        mine = lax.broadcasted_iota(jnp.int32, (count, pairs), 0) == row
        here = lax.broadcasted_iota(jnp.int32, (block_rows, pairs), 0) == lane
        return lax.dot_general(
            jnp.where(mine, code.astype(jnp.float32), 0.0).astype(jnp.bfloat16),
            jnp.where(here, 1.0, 0.0).astype(jnp.bfloat16),
            (((1,), (1,)), ((), ())),
            preferred_element_type=jnp.float32,
        )

    own = code_rows(zl * nz + z, line, plane * CAP + rank)
    both = code_rows(z, nz, (plane * nl + zl) * CAP + rank)
    both = jnp.concatenate([both] * nl, axis=0)
    row = lax.broadcasted_iota(jnp.int32, (line, 1, CAP, block_rows), 2)
    own, both = own[:, None, None, :], both[:, None, None, :]
    out_ref[...] = jnp.concatenate(
        [
            send.reshape(line, groups - 1, CAP, block_rows),
            jnp.where(row == 0, own, both),
        ],
        axis=1,
    ).astype(jnp.bfloat16)


def route(pair_block, pair_protein, pair_weight, line, nl, nh, per_z, proteins):
    pairs, block_rows = pair_weight.shape
    return pl.pallas_call(
        functools.partial(route_kernel, nl, nh, proteins),
        in_specs=[pl.BlockSpec(memory_space=pl.ANY)] * 3,
        out_shape=jax.ShapeDtypeStruct((line, per_z // CAP + 1, CAP, block_rows), jnp.bfloat16),
        scratch_shapes=[
            pltpu.VMEM((1, pairs), jnp.int32),
            pltpu.VMEM((1, pairs), jnp.int32),
            pltpu.VMEM((pairs, block_rows), jnp.bfloat16),
            pltpu.SemaphoreType.DMA((3,)),
        ],
        compiler_params=pltpu.CompilerParams(vmem_limit_bytes=16 * 2**20),
        name="route",
    )(
        pltpu.with_memory_space_constraint(pair_block.reshape(1, pairs), pltpu.HBM),
        pltpu.with_memory_space_constraint(pair_protein.reshape(1, pairs), pltpu.HBM),
        pltpu.with_memory_space_constraint(pair_weight, pltpu.HBM),
    )


def owner_kernel(got_ref, table_ref, partial_ref, dense_ref):
    places, groups, _, block_rows = got_ref.shape
    per_p = (groups - 1) * CAP
    got = got_ref[...].astype(jnp.float32)
    weights = got[:, : groups - 1].reshape(places, per_p, block_rows)
    shape = (places, per_p, block_rows)
    diagonal = lax.broadcasted_iota(jnp.int32, shape, 1) == lax.broadcasted_iota(
        jnp.int32, shape, 2
    )
    row = got[:, groups - 1, :1, :]
    block = jnp.sum(jnp.where(diagonal, row, 0.0), axis=2, keepdims=True)
    for b in range(dense_ref.shape[1] // block_rows):
        mine = jnp.where(block == b, weights, 0.0).astype(jnp.bfloat16)
        dense_ref[:, b * block_rows : (b + 1) * block_rows] = mine.reshape(
            places * per_p, block_rows
        )
    partial_ref[...] = (
        jnp.dot(dense_ref[...], table_ref[...], preferred_element_type=jnp.float32)
        .astype(jnp.bfloat16)
        .reshape(partial_ref.shape)
    )


def update_kernel(dense_ref, grad_ref, accum_ref, table_ref, table_out, accum_out, sum_ref):
    slots = dense_ref.shape[0]
    block_rows = accum_ref.shape[2]
    sum_ref[...] = lax.dot_general(
        dense_ref[...],
        grad_ref[...].reshape(slots, grad_ref.shape[2]),
        (((0,), (0,)), ((), ())),
        preferred_element_type=jnp.float32,
    )
    square = (block_rows, block_rows)
    diagonal = lax.broadcasted_iota(jnp.int32, square, 0) == lax.broadcasted_iota(
        jnp.int32, square, 1
    )
    for b in range(accum_ref.shape[0]):
        rows = slice(b * block_rows, (b + 1) * block_rows)
        grad = sum_ref[rows, :]
        accum = jnp.sum(jnp.where(diagonal, accum_ref[b], 0.0), axis=1, keepdims=True)
        accum = accum + jnp.mean(grad * grad, axis=1, keepdims=True)
        rate = 0.3 / (jnp.sqrt(accum) + 1e-08)
        table_out[rows, :] = (table_ref[rows, :].astype(jnp.float32) - grad * rate).astype(
            jnp.bfloat16
        )
        accum_out[b] = jnp.sum(jnp.where(diagonal, accum, 0.0), axis=0, keepdims=True)


def update_rows(dense, grad, table, accum, block_rows):
    rows_dev, width = table.shape
    blocks = rows_dev // block_rows
    new_table, new_accum = pl.pallas_call(
        update_kernel,
        out_shape=[
            jax.ShapeDtypeStruct(table.shape, table.dtype),
            jax.ShapeDtypeStruct((blocks, 1, block_rows), jnp.float32),
        ],
        scratch_shapes=[pltpu.VMEM((rows_dev, width), jnp.float32)],
        compiler_params=pltpu.CompilerParams(vmem_limit_bytes=24 * 2**20),
        name="update_rows",
    )(dense, grad, accum.reshape(blocks, 1, block_rows), table)
    return new_table, new_accum.reshape(accum.shape)


def owner_partials(got, table, targets):
    slots = got.shape[0] * (got.shape[1] - 1) * CAP
    rows_dev, width = table.shape
    return pl.pallas_call(
        owner_kernel,
        out_shape=[
            jax.ShapeDtypeStruct((targets, slots // targets, width), jnp.bfloat16),
            jax.ShapeDtypeStruct((slots, rows_dev), jnp.bfloat16),
        ],
        compiler_params=pltpu.CompilerParams(vmem_limit_bytes=24 * 2**20),
        name="owner_partials",
    )(got, table)


def membership(codes, first_row, sums, proteins, per_p, slots):
    rows, lanes = codes.shape
    source = lax.broadcasted_iota(jnp.int32, (sums, rows), 0) // proteins + first_row
    spread = source == lax.broadcasted_iota(jnp.int32, (sums, rows), 1)
    by_row = jnp.dot(
        jnp.where(spread, 1.0, 0.0).astype(jnp.bfloat16),
        codes,
        preferred_element_type=jnp.float32,
    ).astype(jnp.bfloat16)
    slot = lax.broadcasted_iota(jnp.int32, (lanes, slots), 1)
    entry = (slot // per_p) * CAP + slot % CAP
    move = lax.broadcasted_iota(jnp.int32, (lanes, slots), 0) == entry
    code = jnp.dot(
        by_row, jnp.where(move, 1.0, 0.0).astype(jnp.bfloat16), preferred_element_type=jnp.float32
    ).astype(jnp.int32)
    row = lax.broadcasted_iota(jnp.int32, (sums, slots), 0)
    slot = lax.broadcasted_iota(jnp.int32, (sums, slots), 1)
    low = (row % proteins) * BLK_DEV
    mine = (row // proteins == (slot % per_p) // CAP) & (code > low) & (code <= low + BLK_DEV)
    return jnp.where(mine, 1.0, 0.0).astype(jnp.bfloat16)


def sum_kernel(codes_ref, got_ref, out_ref, member_ref):
    nz, proteins, _ = out_ref.shape
    _, per_p, width = got_ref.shape
    sums, slots = member_ref.shape
    codes = codes_ref[...].astype(jnp.float32)[:, 1, :].astype(jnp.bfloat16)
    member_ref[...] = membership(
        codes, lax.axis_index("zl") * nz, sums, proteins, per_p, slots
    )
    total = jnp.dot(
        member_ref[...], got_ref[...].reshape(slots, width), preferred_element_type=jnp.float32
    )
    out_ref[...] = total.reshape(out_ref.shape)


def protein_sums(codes, got, nz, proteins):
    npl, per_p, width = got.shape
    return pl.pallas_call(
        sum_kernel,
        out_shape=[
            jax.ShapeDtypeStruct((nz, proteins, width), jnp.float32),
            jax.ShapeDtypeStruct((nz * proteins, npl * per_p), jnp.bfloat16),
        ],
        compiler_params=pltpu.CompilerParams(vmem_limit_bytes=16 * 2**20),
        name="protein_sums",
    )(codes, got)


def select_kernel(member_ref, every_ref, out_ref):
    nz, rows, lanes = every_ref.shape
    width = out_ref.shape[2]
    proteins = rows * lanes // width
    every = every_ref[...].astype(jnp.float32)
    every = jnp.concatenate(
        [
            every[:, j : j + proteins, :].reshape(nz * proteins, lanes)
            for j in range(0, rows, proteins)
        ],
        axis=1,
    )
    picked = lax.dot_general(
        member_ref[...],
        every.astype(jnp.bfloat16),
        (((0,), (0,)), ((), ())),
        preferred_element_type=jnp.float32,
    )
    out_ref[...] = picked.astype(jnp.bfloat16).reshape(out_ref.shape)


def select_grads(member, every, npl, width):
    slots = member.shape[1]
    return pl.pallas_call(
        select_kernel,
        out_shape=jax.ShapeDtypeStruct((npl, slots // npl, width), jnp.bfloat16),
        compiler_params=pltpu.CompilerParams(vmem_limit_bytes=16 * 2**20),
        name="select_grads",
    )(member, every)


def exchange(x, axes):
    return lax.all_to_all(x, axes, split_axis=0, concat_axis=0, tiled=True)


def per_device(table, accum, pair_block, pair_protein, pair_weight, w_hidden, hidden_cot):
    nz, nl, nh = lax.axis_size("z"), lax.axis_size("zl"), lax.axis_size("xh")
    line, plane, group = nz * nl, lax.axis_size(PLANE), lax.axis_size(GROUP)
    block_rows = pair_weight.shape[1]
    proteins, width = hidden_cot.shape
    per_z = plane * CAP
    per_p = line * CAP

    first = route(pair_block, pair_protein, pair_weight, line, nl, nh, per_z, proteins)
    first = exchange(first, LINE)

    weights = first[:, :plane].transpose(1, 0, 2, 3)
    codes = lax.optimization_barrier(first[:, plane])
    code = codes[:, 0, :per_z].astype(jnp.int32).reshape(line, plane, CAP).transpose(1, 0, 2)
    block = ((code - 1) & (BLK_DEV - 1)).astype(jnp.bfloat16).reshape(plane, 1, 1, per_p)
    block = jnp.pad(block, ((0, 0), (0, 0), (0, CAP - 1), (0, block_rows - per_p)))
    second = exchange(jnp.concatenate([weights, block], axis=1), PLANE)
    partial_value, dense = owner_partials(second, table, group)

    sums, member = protein_sums(codes, exchange(partial_value, GROUP), nz, proteins)
    dbag = dense_layer(exchange(sums, "z"), w_hidden, hidden_cot)

    every = exchange(dbag, "z")
    grad = exchange(select_grads(member, every, group, width), GROUP)
    return update_rows(dense, grad, table, accum, block_rows)


def solution(mesh):
    split = Mesh(mesh.devices.reshape(SIZES), AXES)
    in_specs = (
        P(AXES, None),
        P(AXES),
        P(AXES),
        P(AXES),
        P(AXES, None),
        P(),
        P(AXES, None),
    )
    out_specs = (P(AXES, None), P(AXES))
    return jax.shard_map(
        per_device, mesh=split, in_specs=in_specs, out_specs=out_specs, check_vma=False
    )
```

```python
import functools

import jax
import jax.numpy as jnp
from jax import lax
from jax.experimental import pallas as pl
from jax.experimental.pallas import tpu as pltpu
from jax.sharding import Mesh
from jax.sharding import PartitionSpec as P

CAP = 2
BLK_DEV = 4
AXES = ("xl", "y", "c", "z", "zl", "xh")
SIZES = (2, 4, 2, 8, 2, 2)
LINE = ("zl", "z")
PLANE = ("xl", "y", "c", "xh")
GROUP = ("xl", "y", "c", "xh", "zl")


def dense_layer_kernel(sums_ref, w_ref, cot_ref, out_ref):
    nz = sums_ref.shape[0]
    bag = sums_ref[0]
    for z in range(1, nz):
        bag = bag + sums_ref[z]
    inv = lax.rsqrt(jnp.mean(bag * bag, axis=-1, keepdims=True) + 1e-06)
    unit = bag * inv
    pre = jnp.dot(unit.astype(jnp.bfloat16), w_ref[...], preferred_element_type=jnp.float32)
    sig = jax.nn.sigmoid(pre)
    dpre = (cot_ref[...].astype(jnp.float32) * sig * (1.0 + pre * (1.0 - sig))).astype(
        jnp.bfloat16
    )
    dunit = lax.dot_general(
        dpre, w_ref[...], (((1,), (1,)), ((), ())), preferred_element_type=jnp.float32
    )
    dbag = (dunit - unit * jnp.mean(dunit * unit, axis=-1, keepdims=True)) * inv
    lanes = out_ref.shape[2]
    rows = [dbag[:, j : j + lanes] for j in range(0, dbag.shape[1], lanes)]
    message = jnp.concatenate(rows, axis=0).astype(jnp.bfloat16)
    out_ref[...] = jnp.broadcast_to(message[None], out_ref.shape)


def dense_layer(sums, w_hidden, hidden_cot):
    nz, proteins, width = sums.shape
    return pl.pallas_call(
        dense_layer_kernel,
        out_shape=jax.ShapeDtypeStruct((nz, proteins * width // 128, 128), jnp.bfloat16),
        compiler_params=pltpu.CompilerParams(vmem_limit_bytes=16 * 2**20),
        name="dense_layer",
    )(sums, w_hidden, hidden_cot)


def route_kernel(
    nl, nh, proteins, block_in, protein_in, weight_in, out_ref, block_ref, protein_ref, weight_ref, sems
):
    copies = [
        pltpu.make_async_copy(source, target, sems.at[i])
        for i, (source, target) in enumerate(
            [(block_in, block_ref), (protein_in, protein_ref), (weight_in, weight_ref)]
        )
    ]
    for copy in copies:
        copy.start()
    for copy in copies:
        copy.wait()
    line, groups, _, block_rows = out_ref.shape
    pairs = block_ref.shape[1]
    per_z = (groups - 1) * CAP
    slots = line * per_z
    block = block_ref[...]
    owner = block // BLK_DEV
    code = (protein_ref[...] % proteins) * BLK_DEV + block % BLK_DEV + 1

    square = (pairs, pairs)
    down = lax.broadcasted_iota(jnp.int32, square, 0)
    across = lax.broadcasted_iota(jnp.int32, square, 1)
    owner_f = owner.astype(jnp.float32)
    column = jnp.sum(jnp.where(down == across, owner_f, 0.0), axis=1, keepdims=True)
    earlier = jnp.where((column == owner_f) & (down < across), 1.0, 0.0)
    rank = jnp.sum(earlier, axis=0, keepdims=True).astype(jnp.int32)

    n_dp = line * nh
    nz = line // nl
    along = (owner % n_dp) // nh
    z, zl = along // nl, along % nl
    plane = (owner // n_dp) * nh + owner % nh
    place = lax.broadcasted_iota(jnp.int32, (slots, pairs), 0) == (
        (zl * nz + z) * per_z + plane * CAP + rank
    )
    send = jnp.dot(
        jnp.where(place, 1.0, 0.0).astype(jnp.bfloat16),
        weight_ref[...],
        preferred_element_type=jnp.float32,
    )

    def code_rows(row, count, lane):
        mine = lax.broadcasted_iota(jnp.int32, (count, pairs), 0) == row
        here = lax.broadcasted_iota(jnp.int32, (block_rows, pairs), 0) == lane
        return lax.dot_general(
            jnp.where(mine, code.astype(jnp.float32), 0.0).astype(jnp.bfloat16),
            jnp.where(here, 1.0, 0.0).astype(jnp.bfloat16),
            (((1,), (1,)), ((), ())),
            preferred_element_type=jnp.float32,
        )

    own = code_rows(zl * nz + z, line, plane * CAP + rank)
    both = code_rows(z, nz, (plane * nl + zl) * CAP + rank)
    both = jnp.concatenate([both] * nl, axis=0)
    row = lax.broadcasted_iota(jnp.int32, (line, 1, CAP, block_rows), 2)
    own, both = own[:, None, None, :], both[:, None, None, :]
    out_ref[...] = jnp.concatenate(
        [
            send.reshape(line, groups - 1, CAP, block_rows),
            jnp.where(row == 0, own, both),
        ],
        axis=1,
    ).astype(jnp.bfloat16)


def route(pair_block, pair_protein, pair_weight, line, nl, nh, per_z, proteins):
    pairs, block_rows = pair_weight.shape
    return pl.pallas_call(
        functools.partial(route_kernel, nl, nh, proteins),
        in_specs=[pl.BlockSpec(memory_space=pl.ANY)] * 3,
        out_shape=jax.ShapeDtypeStruct((line, per_z // CAP + 1, CAP, block_rows), jnp.bfloat16),
        scratch_shapes=[
            pltpu.VMEM((1, pairs), jnp.int32),
            pltpu.VMEM((1, pairs), jnp.int32),
            pltpu.VMEM((pairs, block_rows), jnp.bfloat16),
            pltpu.SemaphoreType.DMA((3,)),
        ],
        compiler_params=pltpu.CompilerParams(vmem_limit_bytes=16 * 2**20),
        name="route",
    )(
        pltpu.with_memory_space_constraint(pair_block.reshape(1, pairs), pltpu.HBM),
        pltpu.with_memory_space_constraint(pair_protein.reshape(1, pairs), pltpu.HBM),
        pltpu.with_memory_space_constraint(pair_weight, pltpu.HBM),
    )


def forward_kernel(first_ref, out_ref):
    line, groups, _, lanes = first_ref.shape
    plane = groups - 1
    for z in range(line):
        out_ref[:, z] = first_ref[z, :plane]
    code = first_ref[:, plane].astype(jnp.float32)[:, 0, :].astype(jnp.int32)
    block = ((code - 1) & (BLK_DEV - 1)).astype(jnp.float32).astype(jnp.bfloat16)
    rows = jnp.zeros((plane, lanes), jnp.float32)
    for r in range(CAP):
        pick = lax.broadcasted_iota(jnp.int32, (lanes, plane), 0) == (
            lax.broadcasted_iota(jnp.int32, (lanes, plane), 1) * CAP + r
        )
        put = lax.broadcasted_iota(jnp.int32, (line, lanes), 1) == (
            lax.broadcasted_iota(jnp.int32, (line, lanes), 0) * CAP + r
        )
        picked = jnp.dot(
            block, jnp.where(pick, 1.0, 0.0).astype(jnp.bfloat16), preferred_element_type=jnp.float32
        )
        rows = rows + lax.dot_general(
            picked.astype(jnp.bfloat16),
            jnp.where(put, 1.0, 0.0).astype(jnp.bfloat16),
            (((0,), (0,)), ((), ())),
            preferred_element_type=jnp.float32,
        )
    row = lax.broadcasted_iota(jnp.int32, (plane, CAP, lanes), 1)
    out_ref[:, line] = jnp.where(row == 0, rows[:, None, :], 0.0).astype(jnp.bfloat16)


def forward(first):
    line, groups, cap, lanes = first.shape
    return pl.pallas_call(
        forward_kernel,
        out_shape=jax.ShapeDtypeStruct((groups - 1, line + 1, cap, lanes), first.dtype),
        compiler_params=pltpu.CompilerParams(vmem_limit_bytes=16 * 2**20),
        name="forward",
    )(first)


def owner_kernel(got_ref, table_ref, partial_ref, dense_ref):
    places, groups, _, block_rows = got_ref.shape
    per_p = (groups - 1) * CAP
    got = got_ref[...].astype(jnp.float32)
    weights = got[:, : groups - 1].reshape(places, per_p, block_rows)
    shape = (places, per_p, block_rows)
    diagonal = lax.broadcasted_iota(jnp.int32, shape, 1) == lax.broadcasted_iota(
        jnp.int32, shape, 2
    )
    row = got[:, groups - 1, :1, :]
    block = jnp.sum(jnp.where(diagonal, row, 0.0), axis=2, keepdims=True)
    for b in range(dense_ref.shape[1] // block_rows):
        mine = jnp.where(block == b, weights, 0.0).astype(jnp.bfloat16)
        dense_ref[:, b * block_rows : (b + 1) * block_rows] = mine.reshape(
            places * per_p, block_rows
        )
    partial_ref[...] = (
        jnp.dot(dense_ref[...], table_ref[...], preferred_element_type=jnp.float32)
        .astype(jnp.bfloat16)
        .reshape(partial_ref.shape)
    )


def update_kernel(dense_ref, grad_ref, accum_ref, table_ref, table_out, accum_out, sum_ref):
    slots = dense_ref.shape[0]
    block_rows = accum_ref.shape[2]
    sum_ref[...] = lax.dot_general(
        dense_ref[...],
        grad_ref[...].reshape(slots, grad_ref.shape[2]),
        (((0,), (0,)), ((), ())),
        preferred_element_type=jnp.float32,
    )
    square = (block_rows, block_rows)
    diagonal = lax.broadcasted_iota(jnp.int32, square, 0) == lax.broadcasted_iota(
        jnp.int32, square, 1
    )
    for b in range(accum_ref.shape[0]):
        rows = slice(b * block_rows, (b + 1) * block_rows)
        grad = sum_ref[rows, :]
        accum = jnp.sum(jnp.where(diagonal, accum_ref[b], 0.0), axis=1, keepdims=True)
        accum = accum + jnp.mean(grad * grad, axis=1, keepdims=True)
        rate = 0.3 / (jnp.sqrt(accum) + 1e-08)
        table_out[rows, :] = (table_ref[rows, :].astype(jnp.float32) - grad * rate).astype(
            jnp.bfloat16
        )
        accum_out[b] = jnp.sum(jnp.where(diagonal, accum, 0.0), axis=0, keepdims=True)


def update_rows(dense, grad, table, accum, block_rows):
    rows_dev, width = table.shape
    blocks = rows_dev // block_rows
    new_table, new_accum = pl.pallas_call(
        update_kernel,
        out_shape=[
            jax.ShapeDtypeStruct(table.shape, table.dtype),
            jax.ShapeDtypeStruct((blocks, 1, block_rows), jnp.float32),
        ],
        scratch_shapes=[pltpu.VMEM((rows_dev, width), jnp.float32)],
        compiler_params=pltpu.CompilerParams(vmem_limit_bytes=24 * 2**20),
        name="update_rows",
    )(dense, grad, accum.reshape(blocks, 1, block_rows), table)
    return new_table, new_accum.reshape(accum.shape)


def owner_partials(got, table, targets):
    slots = got.shape[0] * (got.shape[1] - 1) * CAP
    rows_dev, width = table.shape
    return pl.pallas_call(
        owner_kernel,
        out_shape=[
            jax.ShapeDtypeStruct((targets, slots // targets, width), jnp.bfloat16),
            jax.ShapeDtypeStruct((slots, rows_dev), jnp.bfloat16),
        ],
        compiler_params=pltpu.CompilerParams(vmem_limit_bytes=24 * 2**20),
        name="owner_partials",
    )(got, table)


def membership(codes, first_row, sums, proteins, per_p, slots):
    rows, lanes = codes.shape
    source = lax.broadcasted_iota(jnp.int32, (sums, rows), 0) // proteins + first_row
    spread = source == lax.broadcasted_iota(jnp.int32, (sums, rows), 1)
    by_row = jnp.dot(
        jnp.where(spread, 1.0, 0.0).astype(jnp.bfloat16),
        codes,
        preferred_element_type=jnp.float32,
    ).astype(jnp.bfloat16)
    slot = lax.broadcasted_iota(jnp.int32, (lanes, slots), 1)
    entry = (slot // per_p) * CAP + slot % CAP
    move = lax.broadcasted_iota(jnp.int32, (lanes, slots), 0) == entry
    code = jnp.dot(
        by_row, jnp.where(move, 1.0, 0.0).astype(jnp.bfloat16), preferred_element_type=jnp.float32
    ).astype(jnp.int32)
    row = lax.broadcasted_iota(jnp.int32, (sums, slots), 0)
    slot = lax.broadcasted_iota(jnp.int32, (sums, slots), 1)
    low = (row % proteins) * BLK_DEV
    mine = (row // proteins == (slot % per_p) // CAP) & (code > low) & (code <= low + BLK_DEV)
    return jnp.where(mine, 1.0, 0.0).astype(jnp.bfloat16)


def sum_kernel(first_ref, got_ref, out_ref, member_ref):
    nz, proteins, _ = out_ref.shape
    _, per_p, width = got_ref.shape
    sums, slots = member_ref.shape
    codes = first_ref[:, first_ref.shape[1] - 1].astype(jnp.float32)[:, 1, :]
    codes = codes.astype(jnp.bfloat16)
    member_ref[...] = membership(
        codes, lax.axis_index("zl") * nz, sums, proteins, per_p, slots
    )
    total = jnp.dot(
        member_ref[...], got_ref[...].reshape(slots, width), preferred_element_type=jnp.float32
    )
    out_ref[...] = total.reshape(out_ref.shape)


def protein_sums(first, got, nz, proteins):
    npl, per_p, width = got.shape
    return pl.pallas_call(
        sum_kernel,
        out_shape=[
            jax.ShapeDtypeStruct((nz, proteins, width), jnp.float32),
            jax.ShapeDtypeStruct((nz * proteins, npl * per_p), jnp.bfloat16),
        ],
        compiler_params=pltpu.CompilerParams(vmem_limit_bytes=16 * 2**20),
        name="protein_sums",
    )(first, got)


def select_kernel(member_ref, every_ref, out_ref):
    nz, rows, lanes = every_ref.shape
    width = out_ref.shape[2]
    proteins = rows * lanes // width
    every = every_ref[...].astype(jnp.float32)
    every = jnp.concatenate(
        [
            every[:, j : j + proteins, :].reshape(nz * proteins, lanes)
            for j in range(0, rows, proteins)
        ],
        axis=1,
    )
    picked = lax.dot_general(
        member_ref[...],
        every.astype(jnp.bfloat16),
        (((0,), (0,)), ((), ())),
        preferred_element_type=jnp.float32,
    )
    out_ref[...] = picked.astype(jnp.bfloat16).reshape(out_ref.shape)


def select_grads(member, every, npl, width):
    slots = member.shape[1]
    return pl.pallas_call(
        select_kernel,
        out_shape=jax.ShapeDtypeStruct((npl, slots // npl, width), jnp.bfloat16),
        compiler_params=pltpu.CompilerParams(vmem_limit_bytes=16 * 2**20),
        name="select_grads",
    )(member, every)


def exchange(x, axes):
    return lax.all_to_all(x, axes, split_axis=0, concat_axis=0, tiled=True)


def per_device(table, accum, pair_block, pair_protein, pair_weight, w_hidden, hidden_cot):
    nz, nl, nh = lax.axis_size("z"), lax.axis_size("zl"), lax.axis_size("xh")
    line, plane, group = nz * nl, lax.axis_size(PLANE), lax.axis_size(GROUP)
    block_rows = pair_weight.shape[1]
    proteins, width = hidden_cot.shape
    per_z = plane * CAP

    first = route(pair_block, pair_protein, pair_weight, line, nl, nh, per_z, proteins)
    first = exchange(first, LINE)

    second = exchange(forward(first), PLANE)
    partial_value, dense = owner_partials(second, table, group)

    sums, member = protein_sums(first, exchange(partial_value, GROUP), nz, proteins)
    dbag = dense_layer(exchange(sums, "z"), w_hidden, hidden_cot)

    every = exchange(dbag, "z")
    grad = exchange(select_grads(member, every, group, width), GROUP)
    return update_rows(dense, grad, table, accum, block_rows)


def solution(mesh):
    split = Mesh(mesh.devices.reshape(SIZES), AXES)
    in_specs = (
        P(AXES, None),
        P(AXES),
        P(AXES),
        P(AXES),
        P(AXES, None),
        P(),
        P(AXES, None),
    )
    out_specs = (P(AXES, None), P(AXES))
    return jax.shard_map(
        per_device, mesh=split, in_specs=in_specs, out_specs=out_specs, check_vma=False
    )
```
